32 devices in a mesh: dp: 4 (over y, x), expert: 8 (over z, core).
Axes of the slice: x: 2, y: 2, z: 4, core: 2. Of those that a mesh axis runs over, the one named last changes fastest.
Arguments:
- tokens: bfloat16 [4096, 2048], P(('dp', 'expert')), may hold values from -6 to 6
- cotangent: bfloat16 [4096, 2048], P(('dp', 'expert')), may hold values from -6 to 6
- routes: int32 [4096, 8], P(('dp', 'expert')), may hold values from 0 to 63, all different within a row; in each aligned block of 128 rows (0 to 127, 128 to 255, ...) at most 18 rows name the same one
- probs: bfloat16 [4096, 8], P(('dp', 'expert')), may hold values from 0.019897461 to 0.29882812
- slot_expert: int32 [64], replicated, may hold values from 0 to 63, each once
- gate_w: bfloat16 [64, 2048, 384], P('expert', 'dp'), may hold values from -0.125 to 0.125
- up_w: bfloat16 [64, 2048, 384], P('expert', 'dp'), may hold values from -0.125 to 0.125
- down_w: bfloat16 [64, 384, 2048], P('expert', None, 'dp'), may hold values from -0.3125 to 0.3125
Outputs:
- grad_tokens: bfloat16 [4096, 2048], P(('dp', 'expert'))
- grad_probs: bfloat16 [4096, 8], P(('dp', 'expert'))
- grad_gate: float32 [64, 2048, 384], P('expert', 'dp')
- grad_up: float32 [64, 2048, 384], P('expert', 'dp')
- grad_down: float32 [64, 384, 2048], P('expert', None, 'dp')
The draws below stay inside these ranges and needn't reach their ends.
Inputs may be any that keep to these rules, and one draw needn't show every extreme that they name: `routes`: in each aligned block of 128 rows (the tokens of one device) no expert is named by more than 18 rows, a bound that some block reaches; a row names 8 different experts. `slot_expert`: each expert stands in exactly one slot.
All inputs are finite; a program needn't handle non-finite values.
Results may differ from the reference program's by a relative error of at most 0.008.
Values may be sent and summed in bfloat16 or wider, within the bound.
No kernel may reach another device: no remote copies, remote signals or barrier semaphores. Data moves between devices by JAX's collectives and lax.ppermute only.
A program may use at most 192 MiB of HBM per device.

```python
import math
import jax
import jax.numpy as jnp
import numpy as np
from jax import lax

D = 2048
FF = 384
EXPERTS = 64
TOPK = 8
TOK_DEV = 128
CAP = 18
TOKENS = 4096


def block_scale(own_key, shape, split, low, high):
    def one(dim, blocks):
        draws = jax.random.uniform(jax.random.fold_in(jax.random.fold_in(own_key, 6), dim), (blocks,), jnp.float32, low / len(split), high / len(split))
        return jnp.repeat(jnp.exp(draws), shape[dim] // blocks).reshape((-1,) + (1,) * (len(shape) - dim - 1))

    factor_of = one(*split[0])
    for cut in split[1:]:
        factor_of = factor_of * one(*cut)
    return factor_of


def routed_block(key, own, number, rows, amount, top, limit, slope):
    sequence = jax.random.permutation(key, amount)
    packed, common = shares(amount, rows * top, limit, slope, True), shares(amount, rows * top, limit, slope, False)
    places = jnp.arange(amount)

    def named(sizes, rotation):
        used = int((sizes > 0).sum())
        fixed = max(1, used // 4)
        passed = fixed + (places - fixed + rotation * (used - fixed)) % max(1, amount - fixed)
        return jnp.zeros((amount,), jnp.int32).at[sequence[jnp.where(places < fixed, places, passed)]].set(jnp.asarray(sizes, jnp.int32))

    sizes = jnp.where(number % 4 == 0, named(packed, number // 4), named(common, number - number // 4 - 1))
    mixed = jax.random.permutation(jax.random.fold_in(own, 3), amount)
    donor, receiver = mixed[0:amount // 2 * 2:2], mixed[1:amount // 2 * 2:2]
    slack = jnp.minimum(sizes[donor] - 1, limit - sizes[receiver]) // 2
    slack = jnp.where((donor == sequence[0]) | (receiver == sequence[0]) | (sizes[receiver] == 0), 0, jnp.maximum(slack, 0))
    passed = jax.random.randint(jax.random.fold_in(own, 4), (amount // 2,), 0, 1 << 20) % (slack + 1)
    sizes = sizes.at[donor].add(-passed).at[receiver].add(passed)
    items = jnp.searchsorted(jnp.cumsum(sizes), jnp.arange(rows * top), side="right").astype(jnp.int32)
    grid = items.reshape(top, rows).T
    grid = grid[jax.random.permutation(jax.random.fold_in(own, 1), rows)]
    rotation = jax.random.randint(jax.random.fold_in(own, 2), (rows, 1), 0, top)
    return jnp.take_along_axis(grid, (jnp.arange(top)[None, :] + rotation) % top, axis=1)


def shares(amount, total, limit, skew, full):
    loads = [(1 << 20) // math.isqrt(rank ** skew) + 1 for rank in range(1, amount + 1)]
    largest = limit if full else min(limit, max(-(-total // amount), total * loads[0] // sum(loads)))
    least = 1 if total - largest >= amount - 1 else 0
    counts, surplus = [largest] + [least] * (amount - 1), total - largest - least * (amount - 1)
    while surplus > 0:
        movable = [i for i in range(1, amount) if counts[i] < largest] or [i for i in range(1, amount) if counts[i] < limit]
        pool, left = sum([loads[i] for i in movable]), surplus
        for i in movable:
            addition = min(limit - counts[i], max(1, left * loads[i] // pool), surplus)
            counts[i] = counts[i] + addition
            surplus = surplus - addition
    return np.array(counts)


def centred(key, extent, scale, reach, pieces=(), kind=jnp.bfloat16):
    array = scale * jax.random.normal(key, extent, jnp.float32)
    if pieces:
        array = array * block_scale(key, extent, pieces, -0.22, 0.18)
    return jnp.clip(array, -reach, reach).astype(kind)


def setup_inputs(seed: int = 0) -> dict:
    streams_of = jax.random.split(jax.random.key(seed), 9)
    tokens = centred(streams_of[0], (TOKENS, D), 1.0, 6.0, ((0, 32),))
    cotangent = centred(streams_of[1], (TOKENS, D), 1.0, 6.0, ((0, 32),))
    routes_keys = jax.random.split(jax.random.fold_in(streams_of[2], 1), TOKENS // TOK_DEV)
    routes_turns = jax.random.permutation(jax.random.fold_in(streams_of[2], 3), TOKENS // TOK_DEV)
    routes = jax.vmap(lambda own, number: routed_block(jax.random.fold_in(streams_of[2], 2), own, number, TOK_DEV, EXPERTS, TOPK, CAP, 2))(routes_keys, routes_turns).reshape((TOKENS, TOPK))
    probs = jnp.clip(0.019897461 + 0.27893066 * jax.random.uniform(streams_of[3], (TOKENS, TOPK), jnp.float32) ** block_scale(streams_of[3], (TOKENS, TOPK), ((0, 32),), -0.2, 0.2), 0.019897461, 0.29882812).astype(jnp.bfloat16)
    slot_expert = jax.random.permutation(streams_of[4], EXPERTS).astype(jnp.int32)
    gate_w = centred(streams_of[5], (EXPERTS, D, FF), D ** -0.5, 0.125, ((0, 8), (1, 4)))
    up_w = centred(streams_of[6], (EXPERTS, D, FF), D ** -0.5, 0.125, ((0, 8), (1, 4)))
    down_w = centred(streams_of[7], (EXPERTS, FF, D), FF ** -0.5, 0.3125, ((0, 8), (2, 4)))
    return dict(tokens=tokens, cotangent=cotangent, routes=routes, probs=probs, slot_expert=slot_expert, gate_w=gate_w, up_w=up_w, down_w=down_w)


def reference(tokens, cotangent, routes, probs, slot_expert, gate_w, up_w, down_w):
    n_src = TOKENS // TOK_DEV
    total = TOKENS * TOPK
    flat = routes.reshape(n_src, TOK_DEV * TOPK).astype(jnp.int32)
    labels = jnp.arange(EXPERTS, dtype=jnp.int32)
    onehot = (flat[:, :, None] == labels[None, None, :]).astype(jnp.int32)
    before = jnp.cumsum(onehot, axis=1) - onehot
    position = jnp.sum(before * onehot, axis=2).astype(jnp.int32)
    assign = jnp.arange(total, dtype=jnp.int32).reshape(n_src, TOK_DEV * TOPK)
    source = jnp.broadcast_to(jnp.arange(n_src, dtype=jnp.int32)[:, None], flat.shape)
    table = jnp.full((EXPERTS, n_src, CAP), total, jnp.int32)
    table = table.at[flat, source, position].set(assign).reshape(EXPERTS, n_src * CAP)
    x_pad = jnp.concatenate([tokens, jnp.zeros((1, D), jnp.bfloat16)], axis=0)
    dy_pad = jnp.concatenate([cotangent, jnp.zeros((1, D), jnp.bfloat16)], axis=0)
    p_pad = jnp.concatenate([probs.reshape(-1), jnp.zeros((1,), jnp.bfloat16)], axis=0)

    def one_slot(carry, slot):
        dx_acc, dp_acc = carry
        expert_id = slot_expert[slot]
        index = table[expert_id]
        token_row = jnp.minimum(index // TOPK, TOKENS).astype(jnp.int32)
        x_rows = x_pad[token_row]
        dy_rows = dy_pad[token_row]
        weight = p_pad[index].astype(jnp.float32)[:, None]
        w_gate = gate_w[slot]
        w_up = up_w[slot]
        w_down = down_w[slot]
        gate = jnp.dot(x_rows, w_gate, preferred_element_type=jnp.float32)
        upval = jnp.dot(x_rows, w_up, preferred_element_type=jnp.float32)
        sig = jax.nn.sigmoid(gate)
        act = gate * sig
        hidden = (act * upval).astype(jnp.bfloat16)
        back = jnp.dot(dy_rows, w_down.T, preferred_element_type=jnp.float32)
        dprob = jnp.sum(hidden.astype(jnp.float32) * back, axis=1).astype(jnp.bfloat16)
        dh = weight * back
        d_gate = (dh * upval * sig * (1.0 + gate * (1.0 - sig))).astype(jnp.bfloat16)
        d_up = (dh * act).astype(jnp.bfloat16)
        dx_rows = (jnp.dot(d_gate, w_gate.T, preferred_element_type=jnp.float32)
                   + jnp.dot(d_up, w_up.T, preferred_element_type=jnp.float32)).astype(jnp.bfloat16)
        wdy = (weight * dy_rows.astype(jnp.float32)).astype(jnp.bfloat16)
        g_gate = jnp.dot(x_rows.T, d_gate, preferred_element_type=jnp.float32)
        g_up = jnp.dot(x_rows.T, d_up, preferred_element_type=jnp.float32)
        g_down = jnp.dot(hidden.T, wdy, preferred_element_type=jnp.float32)
        dx_acc = dx_acc.at[token_row].add(dx_rows.astype(jnp.float32))
        dp_acc = dp_acc.at[index].add(dprob.astype(jnp.float32))
        return (dx_acc, dp_acc), (g_gate, g_up, g_down)

    start = (jnp.zeros((TOKENS + 1, D), jnp.float32), jnp.zeros((total + 1,), jnp.float32))
    (dx_acc, dp_acc), (grad_gate, grad_up, grad_down) = lax.scan(one_slot, start, jnp.arange(EXPERTS, dtype=jnp.int32))
    grad_tokens = dx_acc[:TOKENS].astype(jnp.bfloat16)
    grad_probs = dp_acc[:total].reshape(TOKENS, TOPK).astype(jnp.bfloat16)
    return (grad_tokens, grad_probs, grad_gate, grad_up, grad_down)
```

```python
import functools

import jax
import jax.numpy as jnp
from jax import lax
from jax.experimental import pallas as pl
from jax.experimental.pallas import tpu as pltpu
from jax.sharding import PartitionSpec as P

CAP = 18
F32 = jnp.float32
BF16 = jnp.bfloat16
VMEM_LIMIT = 48 * 1024 * 1024
NT = (((1,), (1,)), ((), ()))
TN = (((0,), (0,)), ((), ()))
NN = (((1,), (0,)), ((), ()))


def mm(a, b, dims=NN):
    return lax.dot_general(a, b, dims, preferred_element_type=F32)


def params():
    return pltpu.CompilerParams(vmem_limit_bytes=VMEM_LIMIT)


def cost(flops, nbytes):
    return pl.CostEstimate(flops=int(flops), bytes_accessed=int(nbytes), transcendentals=0)


def payload_kernel(info, tok, cot, routes, probs, experts, *outs):
    n = info[8]
    rows, width = tok.shape
    wide = width // len(outs)
    lanes = experts.shape[1]
    lane = lax.broadcasted_iota(jnp.int32, (rows, lanes), 1)
    hit = jnp.zeros((rows, lanes), F32)
    val = jnp.zeros((rows, lanes), F32)
    want = experts[...]
    rt = routes[...]
    pr = probs[...].astype(F32)
    for k in range(routes.shape[1]):
        eq = rt[:, k : k + 1] == want
        hit = jnp.where(eq, 1.0, hit)
        val = jnp.where(eq, pr[:, k : k + 1], val)
    before = (
        lax.broadcasted_iota(jnp.int32, (rows, rows), 1)
        < lax.broadcasted_iota(jnp.int32, (rows, rows), 0)
    ).astype(F32).astype(BF16)
    pos = mm(before, hit.astype(BF16))
    pos = jnp.where(hit > 0.5, pos, -1.0)
    meta = jnp.where(lane < lanes // 2, pos, val).astype(BF16)
    for o, out in enumerate(outs):
        at = pl.multiple_of((n ^ o) * wide, wide)
        out[:, :wide] = tok[:, pl.ds(at, wide)]
        out[:, wide : 2 * wide] = cot[:, pl.ds(at, wide)]
        out[:, 2 * wide :] = meta


def payload(info, tokens, cotangent, routes, probs, slot_expert, n_dp):
    rows, width = tokens.shape
    wide = width // n_dp
    twice = jnp.concatenate([slot_expert, slot_expert])[None, :]
    cols = 2 * wide + twice.shape[1]
    return pl.pallas_call(
        payload_kernel,
        in_specs=[pl.BlockSpec(memory_space=pltpu.SMEM)] + [pl.BlockSpec(memory_space=pltpu.VMEM)] * 5,
        out_specs=[pl.BlockSpec(memory_space=pltpu.VMEM)] * n_dp,
        out_shape=[jax.ShapeDtypeStruct((rows, cols), BF16)] * n_dp,
        compiler_params=params(),
        name="payload",
    )(info, tokens, cotangent, routes, probs, twice)


def partial_kernel(n_dp, tok, base, keep, *refs):
    info, own, sib, gate, up, down = refs[:6]
    refs = refs[6:]
    xs, dys, dest_out = refs[:3]
    scr = refs[-1]
    g = pl.program_id(0)
    n, first, core = info[8], info[9], info[10]
    wide = xs.shape[-1]
    lanes = own.shape[1] - 2 * wide
    half = lanes // 2

    @pl.when(g == 0)
    def _():
        for c, src in enumerate((own, sib)):
            for o in range(n_dp):
                table = src[o * tok : (o + 1) * tok, 2 * wide :].astype(F32)
                scr[c * n_dp + o] = table.T

    row = first + info[base + g]
    rows = xs.shape[2]
    dests = []
    weights = []
    for c in range(2):
        for o in range(n_dp):
            pos = scr[c * n_dp + o, pl.ds(row, 1), :]
            off = (((n ^ o) * 2 + (core ^ c)) * CAP).astype(F32)
            dests.append(jnp.where(pos < 0, -1.0, pos + off))
            if keep:
                weights.append(scr[c * n_dp + o, pl.ds(half + row, 1), :])
    dest = jnp.concatenate(dests, axis=1).astype(jnp.int32)
    dest_out[0] = dest
    hot = (lax.broadcasted_iota(jnp.int32, (rows, dest.shape[1]), 0) == dest).astype(F32)
    pick = hot.astype(BF16)
    m = n_dp * tok
    got = mm(pick[:, :m], own[:, : 2 * wide]) + mm(pick[:, m:], sib[:, : 2 * wide])
    got = got.astype(BF16)
    x, dy = got[:, :wide], got[:, wide:]
    xs[0, 0] = x
    dys[0, 0] = dy
    gg = mm(x, gate[0])
    uu = mm(x, up[0])
    rr = mm(dy, down[0], NT)
    f = gg.shape[1]

    def put(out, lead):
        out[lead, :, :f] = gg.astype(out.dtype)
        out[lead, :, f : 2 * f] = uu.astype(out.dtype)
        out[lead, :, 2 * f :] = rr.astype(out.dtype)

    if keep:
        put(refs[3], 0)
        prob_out = refs[4]

        @pl.when(g >= 2)
        def _():
            p = jnp.sum(hot * jnp.concatenate(weights, axis=1), axis=1, keepdims=True)
            prob_out[0] = jnp.broadcast_to(p, prob_out.shape[1:])
    else:
        for q in range(4):

            @pl.when(g == q)
            def _():
                put(refs[3 + q], 0)


def partials(info, own, sib, gate_w, up_w, down_w, bufs, chunk, n_chunk, keep, n_dp, tok):
    local, wide, f = gate_w.shape
    rows = 2 * n_dp * CAP
    base = 4 if keep else 0
    total = 2 * n_dp * tok
    at = lambda g, s: (s[base + g], 0, 0)
    buf_at = lambda g, s: (s[base + g], chunk, 0, 0)
    whole = lambda g, s: (0, 0)
    in_specs = [
        pl.BlockSpec(own.shape, whole),
        pl.BlockSpec(sib.shape, whole),
        pl.BlockSpec((1, wide, f), at),
        pl.BlockSpec((1, wide, f), at),
        pl.BlockSpec((1, f, wide), at),
    ]
    args = [info, own, sib, gate_w, up_w, down_w]
    out_shape = [jax.ShapeDtypeStruct((local, n_chunk, rows, wide), BF16)] * 2
    out_shape += [jax.ShapeDtypeStruct((4, 1, total), jnp.int32)]
    out_specs = [pl.BlockSpec((1, 1, rows, wide), buf_at)] * 2
    out_specs += [pl.BlockSpec((1, 1, total), lambda g, s: (g, 0, 0))]
    aliases = {}
    if bufs is not None:
        in_specs += [pl.BlockSpec(memory_space=pl.ANY)] * 2
        args += list(bufs)
        aliases = {6: 0, 7: 1}
    if keep:
        out_shape += [jax.ShapeDtypeStruct((4, rows, 3 * f), F32), jax.ShapeDtypeStruct((2, rows, 128), F32)]
        out_specs += [
            pl.BlockSpec((1, rows, 3 * f), lambda g, s: (g, 0, 0)),
            pl.BlockSpec((1, rows, 128), lambda g, s: (jnp.maximum(g - 2, 0), 0, 0)),
        ]
    else:
        out_shape += [jax.ShapeDtypeStruct((1, rows, 3 * f), BF16)] * 4
        out_specs += [pl.BlockSpec((1, rows, 3 * f), lambda g, s: (0, 0, 0))] * 4

    def kernel(*refs):
        if bufs is not None:
            refs = refs[:6] + refs[8:]
        partial_kernel(n_dp, tok, base, keep, *refs)

    return pl.pallas_call(
        kernel,
        grid_spec=pltpu.PrefetchScalarGridSpec(
            num_scalar_prefetch=1,
            grid=(4,),
            in_specs=in_specs,
            out_specs=out_specs,
            scratch_shapes=[pltpu.VMEM((2 * n_dp, own.shape[1] - 2 * wide, tok), F32)],
        ),
        out_shape=out_shape,
        input_output_aliases=aliases,
        compiler_params=params(),
        cost_estimate=cost(8 * rows * (total * 2 * wide + wide * 3 * f), 8e6),
        name="partials_keep" if keep else "partials_send",
    )(*args)


def inner_kernel(n_dp, tok, info, keep, raw_a, sum_a, raw_b, sum_b, prob, dest, *refs):
    act, table = refs[-2:]
    n, core = info[8], info[10]
    f = act.shape[1] // 3
    rows = keep.shape[1]
    for h, (raw, summed) in enumerate(((raw_a, sum_a), (raw_b, sum_b))):
        t = keep[2 + h] + raw[0].astype(F32) + summed[0].astype(F32)
        g, u, r = t[:, :f], t[:, f : 2 * f], t[:, 2 * f :]
        sg = jax.nn.sigmoid(g)
        silu = g * sg
        hid = silu * u
        p = prob[h][:, :1]
        pr = p * r
        hb = hid.astype(BF16).astype(F32)
        dprob = jnp.sum(hb * r, axis=1, keepdims=True)
        at = slice(h * rows, (h + 1) * rows)
        act[at, :f] = (pr * u * sg * (1.0 + g * (1.0 - sg))).astype(BF16)
        act[at, f : 2 * f] = (pr * silu).astype(BF16)
        act[at, 2 * f :] = (p * hid).astype(BF16)
        want = dest[2 + h]
        eq = lax.broadcasted_iota(jnp.int32, (rows, want.shape[1]), 0) == want
        line = jnp.sum(jnp.where(eq, dprob, 0.0), axis=0, keepdims=True)
        for c in range(2):
            for o in range(n_dp):
                k = c * n_dp + o
                table[n ^ o, 0, core ^ c, pl.ds(h, 1), :] = line[:, k * tok : (k + 1) * tok]


def inner(info, keep, raw_a, sum_a, raw_b, sum_b, prob, dest, table, chunk, n_chunk, n_dp, tok):
    rows, f3 = keep.shape[1:]
    args = [info, keep, raw_a, sum_a, raw_b, sum_b, prob, dest]
    full = lambda a: pl.BlockSpec(a.shape, lambda g, s: (0,) * a.ndim)
    in_specs = [full(a) for a in args[1:]]
    aliases = {}
    if table is not None:
        args.append(table)
        in_specs.append(pl.BlockSpec(memory_space=pl.ANY))
        aliases = {8: 1}
    return pl.pallas_call(
        functools.partial(inner_kernel, n_dp, tok),
        grid_spec=pltpu.PrefetchScalarGridSpec(
            num_scalar_prefetch=1,
            grid=(1,),
            in_specs=in_specs,
            out_specs=[
                pl.BlockSpec((2 * rows, f3), lambda g, s: (0, 0)),
                pl.BlockSpec((n_dp, 1, 2, 2, tok), lambda g, s: (0, s[11 + chunk], 0, 0, 0)),
            ],
        ),
        out_shape=[
            jax.ShapeDtypeStruct((2 * rows, f3), BF16),
            jax.ShapeDtypeStruct((n_dp, n_chunk, 2, 2, tok), F32),
        ],
        input_output_aliases=aliases,
        compiler_params=params(),
        cost_estimate=cost(2 * rows * f3 * 20, 6e6),
        name="inner",
    )(*args)


def dx_kernel(info, own, from_x, from_y, far_a, far_b, dest_s, dest_k, gate, up, *refs):
    acts, out_own, out_sib, act_s, hot_s, dx_s = refs[-6:]
    g = pl.program_id(0)
    rows = far_a.shape[0]
    f = gate.shape[2]

    @pl.when(g == 0)
    def _():
        act_s[0] = far_a[...]
        act_s[1] = far_b[...]
        act_s[2] = from_x[:rows]
        act_s[3] = from_y[rows:]
        act_s[4] = from_y[:rows]
        act_s[5] = from_x[rows:]
        act_s[6] = own[:rows]
        act_s[7] = own[rows:]

    a = act_s[g]
    acts[0, 0] = a
    back = mm(a[:, :f], gate[0], NT) + mm(a[:, f : 2 * f], up[0], NT)
    at = pl.ds(pl.multiple_of(g * rows, rows), rows)
    dx_s[at, :] = back.astype(BF16)
    want = jnp.where(g < 4, dest_s[jnp.minimum(g, 3)], dest_k[jnp.maximum(g - 4, 0)])
    hot = lax.broadcasted_iota(jnp.int32, (rows, want.shape[1]), 0) == want
    hot_s[at, :] = hot.astype(F32).astype(BF16)

    @pl.when(g == 7)
    def _():
        m = out_own.shape[0]
        out_sib[...] = mm(hot_s[:, m:], dx_s[...], TN).astype(out_sib.dtype)
        out_own[...] = mm(hot_s[:, :m], dx_s[...], TN).astype(out_own.dtype)


def dx_chunk(info, own, from_x, from_y, far_a, far_b, dest_s, dest_k, gate_w, up_w, acts, chunk, n_chunk):
    local, wide, f = gate_w.shape
    rows, f3 = far_a.shape
    total = dest_s.shape[-1]
    args = [info, own, from_x, from_y, far_a, far_b, dest_s, dest_k, gate_w, up_w]
    full = lambda a: pl.BlockSpec(a.shape, lambda g, s: (0,) * a.ndim)
    at = lambda g, s: (s[g], 0, 0)
    in_specs = [full(a) for a in args[1:8]] + [pl.BlockSpec((1, wide, f), at)] * 2
    aliases = {}
    if acts is not None:
        args.append(acts)
        in_specs.append(pl.BlockSpec(memory_space=pl.ANY))
        aliases = {10: 0}
    half = pl.BlockSpec((total // 2, wide), lambda g, s: (0, 0))
    return pl.pallas_call(
        dx_kernel,
        grid_spec=pltpu.PrefetchScalarGridSpec(
            num_scalar_prefetch=1,
            grid=(8,),
            in_specs=in_specs,
            out_specs=[pl.BlockSpec((1, 1, rows, f3), lambda g, s: (s[g], chunk, 0, 0)), half, half],
            scratch_shapes=[
                pltpu.VMEM((8, rows, f3), BF16),
                pltpu.VMEM((8 * rows, total), BF16),
                pltpu.VMEM((8 * rows, wide), BF16),
            ],
        ),
        out_shape=[
            jax.ShapeDtypeStruct((local, n_chunk, rows, f3), BF16),
            jax.ShapeDtypeStruct((total // 2, wide), F32),
            jax.ShapeDtypeStruct((total // 2, wide), BF16),
        ],
        input_output_aliases=aliases,
        compiler_params=params(),
        cost_estimate=cost(2 * 8 * rows * (2 * f * wide + total * wide), 12e6),
        name="dx",
    )(*args)


def grads_kernel(xs, dys, acts, out_gate, out_up, out_down):
    f = out_gate.shape[2]
    flat = lambda ref: ref[0].reshape(-1, ref.shape[-1])
    x, dy, a = flat(xs), flat(dys), flat(acts)
    both = mm(x, a[:, : 2 * f], TN)
    out_gate[0] = both[:, :f]
    out_up[0] = both[:, f:]
    out_down[0] = mm(a[:, 2 * f :], dy, TN)


def grads(xs, dys, acts):
    local, n_chunk, rows, wide = xs.shape
    f = acts.shape[-1] // 3
    spec = lambda a: pl.BlockSpec((1,) + a.shape[1:], lambda g: (g, 0, 0, 0))
    shapes = [(local, wide, f), (local, wide, f), (local, f, wide)]
    return pl.pallas_call(
        grads_kernel,
        grid=(local,),
        in_specs=[spec(xs), spec(dys), spec(acts)],
        out_specs=[pl.BlockSpec((1,) + s[1:], lambda g: (g, 0, 0)) for s in shapes],
        out_shape=[jax.ShapeDtypeStruct(s, F32) for s in shapes],
        compiler_params=params(),
        cost_estimate=cost(6 * local * n_chunk * rows * wide * f, 30e6),
        name="grads",
    )(xs, dys, acts)


def join_kernel(info, *refs):
    out = refs[-1]
    wide = refs[0].shape[1]
    for o, piece in enumerate(refs[:-1]):
        out[:, pl.ds(pl.multiple_of((info[8] ^ o) * wide, wide), wide)] = piece[...]


def join(info, pieces):
    rows, wide = pieces[0].shape
    return pl.pallas_call(
        join_kernel,
        in_specs=[pl.BlockSpec(memory_space=pltpu.SMEM)] + [pl.BlockSpec(memory_space=pltpu.VMEM)] * len(pieces),
        out_specs=pl.BlockSpec(memory_space=pltpu.VMEM),
        out_shape=jax.ShapeDtypeStruct((rows, wide * len(pieces)), BF16),
        compiler_params=params(),
        name="join",
    )(info, *pieces)


def shards_rows(tokens, cotangent, routes, probs, slot_expert, gate_w, up_w, down_w):
    n_dp, n_exp = lax.axis_size("dp"), lax.axis_size("expert")
    local = gate_w.shape[0]
    tok = tokens.shape[0]
    n_chunk = n_exp // 2
    rows = 2 * n_dp * CAP
    n, e = lax.axis_index("dp"), lax.axis_index("expert")
    order = [3, 7, 1, 6, 2, 5, 0, 4]
    info = jnp.stack(
        [2 * (n ^ (k % 4)) + k // 4 for k in order]
        + [n, e * local, e % 2]
        + [(e // 2 - j) % n_chunk for j in range(n_chunk)]
    ).astype(jnp.int32)

    def swap(a, o):
        return lax.ppermute(a, "dp", [(k, k ^ o) for k in range(n_dp)])

    def sibling(a):
        return lax.ppermute(a, "expert", [(k, k ^ 1) for k in range(n_exp)])

    def plane(a):
        return lax.ppermute(a, "expert", [(k, (k + 2) % n_exp) for k in range(n_exp)])

    sends = payload(info, tokens, cotangent, routes, probs, slot_expert, n_dp)
    own = jnp.concatenate([sends[0]] + [swap(sends[o], o) for o in range(1, n_dp)], axis=0)

    xy_bufs, acts, table = None, None, None
    home, ring = None, None
    for j in range(n_chunk):
        sib = sibling(own)
        xs, dys, dest_s, a3, b3, a1, b2 = partials(
            info, own, sib, gate_w, up_w, down_w, xy_bufs, j, n_chunk, False, n_dp, tok
        )
        got_a3, got_b3 = swap(a3, 1), swap(b3, 2)
        raw_a, raw_b = swap(a1, 1), swap(b2, 2)
        xs, dys, dest_k, keep, prob = partials(
            info, own, sib, gate_w, up_w, down_w, (xs, dys), j, n_chunk, True, n_dp, tok
        )
        xy_bufs = (xs, dys)
        if j + 1 < n_chunk:
            own = plane(own)
        sum_a = swap((keep[0:1] + got_a3.astype(F32)).astype(BF16), 2)
        sum_b = swap((keep[1:2] + got_b3.astype(F32)).astype(BF16), 1)
        act, table = inner(
            info, keep, raw_a, sum_a, raw_b, sum_b, prob, dest_k, table, j, n_chunk, n_dp, tok
        )
        from_x, from_y = swap(act, 1), swap(act, 2)
        far_a, far_b = swap(from_y[:rows], 1), swap(from_x[rows:], 2)
        acts, dx_own, dx_sib = dx_chunk(
            info, act, from_x, from_y, far_a, far_b, dest_s, dest_k, gate_w, up_w, acts, j, n_chunk
        )
        dx = dx_own + sibling(dx_sib).astype(F32)
        if j == 0:
            home = dx
        else:
            if ring is not None:
                dx = dx + ring.astype(F32)
            ring = plane(dx.astype(BF16))
    grad_gate, grad_up, grad_down = grads(xs, dys, acts)
    if ring is not None:
        home = home + ring.astype(F32)
    home = home.astype(BF16)
    pieces = [home[o * tok : (o + 1) * tok] for o in range(n_dp)]
    grad_tokens = join(info, [pieces[0]] + [swap(pieces[o], o) for o in range(1, n_dp)])
    flat = table.astype(BF16).reshape(n_dp * n_exp, 2, tok)
    flat = lax.all_to_all(flat, ("dp", "expert"), 0, 0, tiled=True)
    by_slot = flat.reshape(n_dp, n_exp, 2, tok).transpose(1, 0, 2, 3).reshape(n_exp * local, tok)
    match = routes[:, :, None] == slot_expert[None, None, :]
    grad_probs = jnp.sum(jnp.where(match, by_slot.T[:, None, :], jnp.zeros((), BF16)), axis=2)
    return (grad_tokens, grad_probs, grad_gate, grad_up, grad_down)


def forward_part(got_x, w_gate, w_up):
    gate = jnp.einsum("sekd,edf->sekf", got_x, w_gate, preferred_element_type=jnp.float32)
    upval = jnp.einsum("sekd,edf->sekf", got_x, w_up, preferred_element_type=jnp.float32)
    sig = jax.nn.sigmoid(gate)
    act = gate * sig
    hidden = (act * upval).astype(jnp.bfloat16)
    return (gate, upval, sig, act, hidden)


def shards_weights(tokens, cotangent, routes, probs, slot_expert, gate_w, up_w, down_w):
    n_exp = lax.axis_size("expert")
    local = gate_w.shape[0]
    tok_rows = tokens.shape[0]
    top = routes.shape[1]
    width = tokens.shape[1]
    count = local * n_exp
    rows_all = count * CAP
    flat = routes.reshape(-1)
    labels = jnp.arange(count, dtype=jnp.int32)
    match = slot_expert[None, :] == labels[:, None]
    slot_of = jnp.sum(jnp.where(match, labels[None, :], 0), axis=1)
    picked = flat[:, None] == labels[None, :]
    target = jnp.sum(jnp.where(picked, slot_of[None, :], 0), axis=1)
    hits = picked.astype(jnp.int32)
    position = jnp.sum((jnp.cumsum(hits, axis=0) - hits) * hits, axis=1)
    where_row = target * CAP + position
    placed = where_row[None, :] == jnp.arange(rows_all, dtype=jnp.int32)[:, None]
    token_map = jnp.any(placed.reshape(rows_all, tok_rows, top), axis=2).astype(jnp.bfloat16)
    send_x = jnp.dot(token_map, tokens, preferred_element_type=jnp.float32).astype(jnp.bfloat16)
    send_x = send_x.reshape(n_exp, local * CAP, width)
    send_dy = jnp.dot(token_map, cotangent, preferred_element_type=jnp.float32).astype(jnp.bfloat16)
    send_dy = send_dy.reshape(n_exp, local * CAP, width)
    zero_p = jnp.zeros((), jnp.bfloat16)
    send_p = jnp.sum(jnp.where(placed, probs.reshape(-1)[None, :], zero_p), axis=1).reshape(
        n_exp, local * CAP
    )
    w_gate, w_up, w_down = (
        lax.all_gather(gate_w, "dp", axis=1, tiled=True),
        lax.all_gather(up_w, "dp", axis=1, tiled=True),
        lax.all_gather(down_w, "dp", axis=2, tiled=True),
    )
    shape_rows = (n_exp, local, CAP, width)
    got_x = lax.all_to_all(send_x, "expert", split_axis=0, concat_axis=0, tiled=True).reshape(
        shape_rows
    )
    gate, upval, sig, act, hidden = forward_part(got_x, w_gate, w_up)
    got_dy, got_p = (
        lax.all_to_all(send_dy, "expert", split_axis=0, concat_axis=0, tiled=True),
        lax.all_to_all(send_p, "expert", split_axis=0, concat_axis=0, tiled=True),
    )
    got_dy = got_dy.reshape(shape_rows)
    weight = got_p.reshape(n_exp, local, CAP).astype(jnp.float32)[..., None]
    back = jnp.einsum("sekd,efd->sekf", got_dy, w_down, preferred_element_type=jnp.float32)
    dprob = jnp.sum(hidden.astype(jnp.float32) * back, axis=-1).astype(jnp.bfloat16)
    dh = weight * back
    d_gate = (dh * upval * sig * (1.0 + gate * (1.0 - sig))).astype(jnp.bfloat16)
    d_up = (dh * act).astype(jnp.bfloat16)
    dx_rows = (
        jnp.einsum("sekf,edf->sekd", d_gate, w_gate, preferred_element_type=jnp.float32)
        + jnp.einsum("sekf,edf->sekd", d_up, w_up, preferred_element_type=jnp.float32)
    ).astype(jnp.bfloat16)
    back_x, back_p = (
        lax.all_to_all(
            dx_rows.reshape(n_exp, local * CAP, width),
            "expert",
            split_axis=0,
            concat_axis=0,
            tiled=True,
        ),
        lax.all_to_all(
            dprob.reshape(n_exp, local * CAP), "expert", split_axis=0, concat_axis=0, tiled=True
        ),
    )
    wdy = (weight * got_dy.astype(jnp.float32)).astype(jnp.bfloat16)
    part_gate = jnp.einsum("sekd,sekf->edf", got_x, d_gate, preferred_element_type=jnp.float32)
    part_up = jnp.einsum("sekd,sekf->edf", got_x, d_up, preferred_element_type=jnp.float32)
    part_down = jnp.einsum("sekf,sekd->efd", hidden, wdy, preferred_element_type=jnp.float32)
    grad_gate, grad_up, grad_down = (
        lax.psum_scatter(part_gate, "dp", scatter_dimension=1, tiled=True),
        lax.psum_scatter(part_up, "dp", scatter_dimension=1, tiled=True),
        lax.psum_scatter(part_down, "dp", scatter_dimension=2, tiled=True),
    )
    returned_rows = back_x.reshape(rows_all, width)
    grad_tokens = lax.dot_general(
        token_map, returned_rows, (((0,), (0,)), ((), ())), preferred_element_type=jnp.float32
    ).astype(jnp.bfloat16)
    grad_probs = jnp.sum(jnp.where(placed, back_p.reshape(rows_all)[:, None], zero_p), axis=0)
    grad_probs = grad_probs.reshape(tok_rows, top)
    return (grad_tokens, grad_probs, grad_gate, grad_up, grad_down)


def solution(mesh):
    placed = (
        P(("dp", "expert"), None),
        P(("dp", "expert"), None),
        P(("dp", "expert"), None),
        P(("dp", "expert"), None),
        P(),
        P("expert", "dp", None),
        P("expert", "dp", None),
        P("expert", None, "dp"),
    )
    n_dp, n_exp = mesh.shape["dp"], mesh.shape["expert"]

    def shards(*args):
        local, rows = args[5].shape[0], 2 * n_dp * CAP
        by_rows = n_dp == 4 and local == 2 * n_dp and n_exp % 2 == 0 and n_exp > 2 and rows % 16 == 0
        return (shards_rows if by_rows else shards_weights)(*args)

    return jax.shard_map(
        shards,
        mesh=mesh,
        in_specs=placed,
        out_specs=(
            P(("dp", "expert"), None),
            P(("dp", "expert"), None),
            P("expert", "dp", None),
            P("expert", "dp", None),
            P("expert", None, "dp"),
        ),
        check_vma=False,
    )
```

```python
import functools

import jax
import jax.numpy as jnp
from jax import lax
from jax.experimental import pallas as pl
from jax.experimental.pallas import tpu as pltpu
from jax.sharding import PartitionSpec as P

CAP = 18
F32 = jnp.float32
BF16 = jnp.bfloat16
VMEM_LIMIT = 20 * 1024 * 1024
GRADS_LIMIT = 56 * 1024 * 1024
NT = (((1,), (1,)), ((), ()))
TN = (((0,), (0,)), ((), ()))
NN = (((1,), (0,)), ((), ()))
IN_SMEM = pl.BlockSpec(memory_space=pltpu.SMEM)
IN_VMEM = pl.BlockSpec(memory_space=pltpu.VMEM)
IN_HBM = pl.BlockSpec(memory_space=pltpu.HBM)


def mm(a, b, dims=NN):
    return lax.dot_general(a, b, dims, preferred_element_type=F32)


def params(limit=VMEM_LIMIT):
    return pltpu.CompilerParams(vmem_limit_bytes=limit)


def cost(flops, nbytes):
    return pl.CostEstimate(flops=int(flops) // 1000, bytes_accessed=int(nbytes) // 1000, transcendentals=0)


def payload_kernel(info, tok, cot, routes, probs, experts, *outs):
    n = info[8]
    rows, width = tok.shape
    wide = width // len(outs)
    lanes = experts.shape[1]
    lane = lax.broadcasted_iota(jnp.int32, (rows, lanes), 1)
    hit = jnp.zeros((rows, lanes), F32)
    val = jnp.zeros((rows, lanes), F32)
    want = experts[...]
    rt = routes[...]
    pr = probs[...].astype(F32)
    for k in range(routes.shape[1]):
        eq = rt[:, k : k + 1] == want
        hit = jnp.where(eq, 1.0, hit)
        val = jnp.where(eq, pr[:, k : k + 1], val)
    before = (
        lax.broadcasted_iota(jnp.int32, (rows, rows), 1)
        < lax.broadcasted_iota(jnp.int32, (rows, rows), 0)
    ).astype(F32).astype(BF16)
    pos = mm(before, hit.astype(BF16))
    pos = jnp.where(hit > 0.5, pos, -1.0)
    meta = jnp.where(lane < lanes // 2, pos, val).astype(BF16)
    for o, out in enumerate(outs):
        at = pl.multiple_of((n ^ o) * wide, wide)
        out[:, :wide] = tok[:, pl.ds(at, wide)]
        out[:, wide : 2 * wide] = cot[:, pl.ds(at, wide)]
        out[:, 2 * wide :] = meta


def payload(info, tokens, cotangent, routes, probs, slot_expert, n_dp):
    rows, width = tokens.shape
    wide = width // n_dp
    twice = jnp.concatenate([slot_expert, slot_expert])[None, :]
    cols = 2 * wide + twice.shape[1]
    return pl.pallas_call(
        payload_kernel,
        in_specs=[pl.BlockSpec(memory_space=pltpu.SMEM)] + [pl.BlockSpec(memory_space=pltpu.VMEM)] * 5,
        out_specs=[pl.BlockSpec(memory_space=pltpu.VMEM)] * n_dp,
        out_shape=[jax.ShapeDtypeStruct((rows, cols), BF16)] * n_dp,
        compiler_params=params(),
        name="payload",
    )(info, tokens, cotangent, routes, probs, twice)


def some_slots(info, base, own, sib, gate, up, down, dest, xs_out, dys_out, pick, xs, dys, sems, put):
    rows, wide = xs.shape[1:]
    m = own.shape[0]
    for q in range(4):
        hot = lax.broadcasted_iota(jnp.int32, (rows, 2 * m), 0) == dest[base + q]
        pick[q * rows : (q + 1) * rows, :] = hot.astype(F32).astype(BF16)
    for k, buf in enumerate((xs, dys)):
        at = slice(k * wide, (k + 1) * wide)
        part = mm(pick[:, :m], own[:, at]) + mm(pick[:, m:], sib[:, at])
        for q in range(4):
            buf[q] = part[q * rows : (q + 1) * rows].astype(BF16)
    copies = [
        pltpu.make_async_copy(xs, xs_out, sems.at[0]),
        pltpu.make_async_copy(dys, dys_out, sems.at[1]),
    ]
    for copy in copies:
        copy.start()
    for q in range(4):
        slot = info[base + q]
        put(q, 0, mm(xs[q], gate[slot]))
        put(q, 1, mm(xs[q], up[slot]))
        put(q, 2, mm(dys[q], down[slot], NT))
    for copy in copies:
        copy.wait()


def send_kernel(n_dp, info, own, sib, gate, up, down, *refs):
    xs_out, dys_out, dest, prob, a3, b3, a1, b2, scr, pick, xs, dys, sems = refs
    n, first, core = info[8], info[9], info[10]
    wide = xs.shape[-1]
    half = scr.shape[1] // 2
    tok = own.shape[0] // n_dp
    f = gate.shape[2]
    for c, src in enumerate((own, sib)):
        for o in range(n_dp):
            scr[c * n_dp + o] = src[o * tok : (o + 1) * tok, 2 * wide :].astype(F32).T
    for q in range(8):
        row = first + info[q]
        for c in range(2):
            for o in range(n_dp):
                k = c * n_dp + o
                at = slice(k * tok, (k + 1) * tok)
                pos = scr[k, pl.ds(row, 1), :]
                off = (((n ^ o) * 2 + (core ^ c)) * CAP).astype(F32)
                dest[q, :, at] = jnp.where(pos < 0, -1.0, pos + off).astype(jnp.int32)
                if q >= 6:
                    prob[q - 6, :, at] = scr[k, pl.ds(half + row, 1), :]

    def put(q, part, value):
        (a3, b3, a1, b2)[q][:, part * f : (part + 1) * f] = value.astype(BF16)

    some_slots(info, 0, own, sib, gate, up, down, dest, xs_out, dys_out, pick, xs, dys, sems, put)


def keep_kernel(n_dp, info, own, sib, gate, up, down, dest, prob, *refs):
    xs_out, dys_out, keep, weight, pick, xs, dys, sems = refs
    f = gate.shape[2]

    def put(q, part, value):
        keep[q, :, part * f : (part + 1) * f] = value

    for h in range(2):
        hot = lax.broadcasted_iota(jnp.int32, (keep.shape[1], dest.shape[2]), 0) == dest[6 + h]
        p = jnp.sum(jnp.where(hot, prob[h], 0.0), axis=1, keepdims=True)
        weight[h] = jnp.broadcast_to(p, weight.shape[1:])
    some_slots(info, 4, own, sib, gate, up, down, dest, xs_out, dys_out, pick, xs, dys, sems, put)


def partials(kernel, info, own, sib, weights, small, n_dp):
    wide, f = weights[0].shape[1:]
    rows = 2 * n_dp * CAP
    m = own.shape[0]
    args = [info, own, sib, *weights, *small]
    out_shape = [jax.ShapeDtypeStruct((4, rows, wide), BF16)] * 2
    scratch = [pltpu.VMEM((4 * rows, 2 * m), BF16)]
    scratch += [pltpu.VMEM((4, rows, wide), BF16)] * 2 + [pltpu.SemaphoreType.DMA((2,))]
    if small:
        out_shape += [jax.ShapeDtypeStruct((4, rows, 3 * f), F32), jax.ShapeDtypeStruct((2, rows, 128), F32)]
    else:
        out_shape += [jax.ShapeDtypeStruct((8, 1, 2 * m), jnp.int32), jax.ShapeDtypeStruct((2, 1, 2 * m), F32)]
        out_shape += [jax.ShapeDtypeStruct((rows, 3 * f), BF16)] * 4
        scratch = [pltpu.VMEM((2 * n_dp, own.shape[1] - 2 * wide, m // n_dp), F32)] + scratch
    return pl.pallas_call(
        functools.partial(kernel, n_dp),
        in_specs=[IN_SMEM] + [IN_VMEM] * (len(args) - 1),
        out_specs=[IN_HBM] * 2 + [IN_VMEM] * (len(out_shape) - 2),
        scratch_shapes=scratch,
        out_shape=out_shape,
        compiler_params=params(),
        cost_estimate=cost(8 * rows * (2 * m * 2 * wide + wide * 3 * f), 8e6),
        name="partials_keep" if small else "partials_send",
    )(*args)


def sums_kernel(keep, got_a, got_b, raw_a, raw_b, to_x, to_y):
    to_x[0] = raw_a[...]
    to_x[1] = (keep[1] + got_b[...].astype(F32)).astype(BF16)
    to_y[0] = (keep[0] + got_a[...].astype(F32)).astype(BF16)
    to_y[1] = raw_b[...]


def second(keep, got_a, got_b, raw_a, raw_b):
    return pl.pallas_call(
        sums_kernel,
        in_specs=[IN_VMEM] * 5,
        out_specs=[IN_VMEM] * 2,
        out_shape=[jax.ShapeDtypeStruct((2,) + raw_a.shape, BF16)] * 2,
        compiler_params=params(),
        cost_estimate=cost(2 * raw_a.size, 4e6),
        name="sums",
    )(keep, got_a, got_b, raw_a, raw_b)


def inner_kernel(keep, got_x, got_y, prob, dest, act, line):
    f = act.shape[1] // 3
    rows = keep.shape[1]
    for h in range(2):
        t = keep[2 + h] + got_x[h].astype(F32) + got_y[h].astype(F32)
        g, u, r = t[:, :f], t[:, f : 2 * f], t[:, 2 * f :]
        sg = jax.nn.sigmoid(g)
        silu = g * sg
        hid = silu * u
        p = prob[h][:, :1]
        pr = p * r
        hb = hid.astype(BF16).astype(F32)
        dprob = jnp.sum(hb * r, axis=1, keepdims=True)
        at = slice(h * rows, (h + 1) * rows)
        act[at, :f] = (pr * u * sg * (1.0 + g * (1.0 - sg))).astype(BF16)
        act[at, f : 2 * f] = (pr * silu).astype(BF16)
        act[at, 2 * f :] = (p * hid).astype(BF16)
        want = dest[6 + h]
        eq = lax.broadcasted_iota(jnp.int32, (rows, want.shape[1]), 0) == want
        line[pl.ds(h, 1), :] = jnp.sum(jnp.where(eq, dprob, 0.0), axis=0, keepdims=True)


def inner(keep, got_x, got_y, prob, dest):
    rows, f3 = keep.shape[1:]
    return pl.pallas_call(
        inner_kernel,
        in_specs=[IN_VMEM] * 5,
        out_specs=[IN_VMEM] * 2,
        out_shape=[
            jax.ShapeDtypeStruct((2 * rows, f3), BF16),
            jax.ShapeDtypeStruct((2, dest.shape[2]), F32),
        ],
        compiler_params=params(),
        cost_estimate=cost(2 * rows * f3 * 20, 6e6),
        name="inner",
    )(keep, got_x, got_y, prob, dest)


def in_order(own, from_x, from_y, far_a, far_b):
    rows = far_a.shape[0]
    return [
        (far_a, 0),
        (far_b, 0),
        (from_x, 0),
        (from_y, rows),
        (from_y, 0),
        (from_x, rows),
        (own, 0),
        (own, rows),
    ]


def dx_kernel(info, own, from_x, from_y, far_a, far_b, dest, gate, up, line, out_own, out_sib, hot_s, dx_s):
    rows = far_a.shape[0]
    f = gate.shape[2]
    m = out_own.shape[1]
    pieces = in_order(own, from_x, from_y, far_a, far_b)
    for q, (ref, lo) in enumerate(pieces):
        a = ref[lo : lo + rows, : 2 * f]
        at = slice(q * rows, (q + 1) * rows)
        back = mm(a[:, :f], gate[info[q]], NT) + mm(a[:, f:], up[info[q]], NT)
        dx_s[at, :] = back.astype(BF16)
        hot = lax.broadcasted_iota(jnp.int32, (rows, 2 * m), 0) == dest[q]
        hot_s[at, :] = hot.astype(F32).astype(BF16)
    wide = dx_s.shape[1]
    extra = out_own.shape[0] - wide
    row = lax.broadcasted_iota(jnp.int32, (extra, 2 * m), 0) - 2 * info[11]
    lines = jnp.where(row == 0, line[0:1, :], jnp.where(row == 1, line[1:2, :], 0.0))
    for c, out in enumerate((out_own, out_sib)):
        at = slice(c * m, (c + 1) * m)
        out[:wide, :] = mm(dx_s[...], hot_s[:, at], TN).astype(out.dtype)
        out[wide:, :] = lines[:, at].astype(out.dtype)


def dx_chunk(info, own, from_x, from_y, far_a, far_b, dest, gate_w, up_w, line, extra):
    wide, f = gate_w.shape[1:]
    rows = far_a.shape[0]
    total = dest.shape[-1]
    return pl.pallas_call(
        dx_kernel,
        in_specs=[IN_SMEM] + [IN_VMEM] * 9,
        out_specs=[IN_VMEM, IN_VMEM],
        scratch_shapes=[pltpu.VMEM((8 * rows, total), BF16), pltpu.VMEM((8 * rows, wide), BF16)],
        out_shape=[
            jax.ShapeDtypeStruct((wide + extra, total // 2), F32),
            jax.ShapeDtypeStruct((wide + extra, total // 2), BF16),
        ],
        compiler_params=params(),
        cost_estimate=cost(2 * 8 * rows * (2 * f * wide + total * wide), 12e6),
        name="dx",
    )(info, own, from_x, from_y, far_a, far_b, dest, gate_w, up_w, line)


def grads_kernel(n_chunk, is_in, info, *refs):
    halves, acts = refs[: 2 * n_chunk], refs[2 * n_chunk : 7 * n_chunk]
    outs, (row_s, act_s) = refs[7 * n_chunk : -2], refs[-2:]
    rows = act_s.shape[0] // n_chunk
    for q in range(8):

        @pl.when(pl.program_id(0) == q)
        def _():
            for k in range(n_chunk):
                at = slice(k * rows, (k + 1) * rows)
                own, from_x, from_y, far_a, far_b = acts[5 * k : 5 * k + 5]
                row_s[at, :] = halves[2 * k + q // 4][0]
                act_s[at, :] = (far_a, far_b, from_x, from_y, from_y, from_x, own, own)[q][...]

    if is_in:
        both = mm(row_s[...], act_s[...], TN)
        f = both.shape[1] // 2
        outs[0][0] = both[:, :f]
        outs[1][0] = both[:, f:]
    else:
        outs[0][0] = mm(act_s[...], row_s[...], TN)


def grads(info, halves, acts, shapes):
    n_chunk = len(halves) // 2
    is_in = len(shapes) == 2
    rows, wide = halves[0].shape[1:]
    cols = acts[0].shape[1] // 3 * len(shapes)
    col = 0 if is_in else 2
    half_specs = [
        pl.BlockSpec((1, rows, wide), lambda g, s: (jnp.minimum(g, 3), 0, 0)),
        pl.BlockSpec((1, rows, wide), lambda g, s: (jnp.maximum(g - 4, 0), 0, 0)),
    ]
    act_specs = [
        pl.BlockSpec((rows, cols), lambda g, s: (jnp.where(g >= 7, 1, 0), col)),
        pl.BlockSpec((rows, cols), lambda g, s: (jnp.where(g >= 5, 1, 0), col)),
        pl.BlockSpec((rows, cols), lambda g, s: (jnp.where(g < 4, 1, 0), col)),
        pl.BlockSpec((rows, cols), lambda g, s: (0, col)),
        pl.BlockSpec((rows, cols), lambda g, s: (0, col)),
    ]
    return pl.pallas_call(
        functools.partial(grads_kernel, n_chunk, is_in),
        grid_spec=pltpu.PrefetchScalarGridSpec(
            num_scalar_prefetch=1,
            grid=(8,),
            in_specs=half_specs * n_chunk + act_specs * n_chunk,
            out_specs=[pl.BlockSpec((1,) + s[1:], lambda g, s: (s[g], 0, 0)) for s in shapes],
            scratch_shapes=[
                pltpu.VMEM((n_chunk * rows, wide), BF16),
                pltpu.VMEM((n_chunk * rows, cols), BF16),
            ],
        ),
        out_shape=[jax.ShapeDtypeStruct(s, F32) for s in shapes],
        compiler_params=params(GRADS_LIMIT),
        cost_estimate=cost(1000 * 16 * n_chunk * rows * wide * cols, 2e10),
        name="grads_in" if is_in else "grads_out",
    )(info, *halves, *acts)


def ready_kernel(gate, up, down, out):
    out[...] = gate[0, :8, :128].astype(F32) + up[0, :8, :128].astype(F32) + down[0, :8, :128].astype(F32)


def ready(weights):
    return pl.pallas_call(
        ready_kernel,
        in_specs=[IN_VMEM] * 3,
        out_specs=IN_VMEM,
        out_shape=jax.ShapeDtypeStruct((8, 128), F32),
        compiler_params=params(),
        name="ready",
    )(*weights)


def join_kernel(info, *refs):
    out, table = refs[-2:]
    wide = out.shape[1] // (len(refs) - 2)
    for o, piece in enumerate(refs[:-2]):
        at = pl.ds(pl.multiple_of((info[8] ^ o) * wide, wide), wide)
        out[:, at] = piece[:wide, :].astype(F32).T.astype(BF16)
        table[info[8] ^ o] = piece[wide:, :].astype(F32)


def join(info, pieces, extra):
    wide, rows = pieces[0].shape[0] - extra, pieces[0].shape[1]
    return pl.pallas_call(
        join_kernel,
        in_specs=[IN_SMEM] + [IN_VMEM] * len(pieces),
        out_specs=[IN_VMEM] * 2,
        out_shape=[
            jax.ShapeDtypeStruct((rows, wide * len(pieces)), BF16),
            jax.ShapeDtypeStruct((len(pieces), extra, rows), F32),
        ],
        compiler_params=params(),
        name="join",
    )(info, *pieces)


def shards_rows(tokens, cotangent, routes, probs, slot_expert, gate_w, up_w, down_w):
    n_dp, n_exp = lax.axis_size("dp"), lax.axis_size("expert")
    local = gate_w.shape[0]
    tok = tokens.shape[0]
    n_chunk = n_exp // 2
    rows = 2 * n_dp * CAP
    n, e = lax.axis_index("dp"), lax.axis_index("expert")
    order = [3, 7, 1, 6, 2, 5, 0, 4]
    info = jnp.stack(
        [2 * (n ^ (k % 4)) + k // 4 for k in order]
        + [n, e * local, e % 2, e]
    ).astype(jnp.int32)

    def swap(a, o):
        return lax.ppermute(a, "dp", [(k, k ^ o) for k in range(n_dp)])

    def sibling(a):
        return lax.ppermute(a, "expert", [(k, k ^ 1) for k in range(n_exp)])

    def after(a, b):
        return lax.optimization_barrier((a, b))[0]

    def plane(a):
        return lax.ppermute(a, "expert", [(k, (k + 2) % n_exp) for k in range(n_exp)])

    last = info

    def now(*arrays):
        out = after(tuple(arrays), last)
        return out if len(out) > 1 else out[0]

    weights = (gate_w, up_w, down_w)
    sends = payload(info, tokens, cotangent, routes, probs, slot_expert, n_dp)
    weights = after(weights, sends[0])
    first = after(sends[0], ready(weights))
    own = jnp.concatenate([first] + [swap(sends[o], o) for o in range(1, n_dp)], axis=0)
    home, ring = None, None
    state = [dict() for _ in range(n_chunk)]

    def take(j):
        nonlocal last
        s = state[j]
        s["own"] = now(s["came"])
        if j + 1 < n_chunk:
            state[j + 1]["came"] = plane(s["own"])
        last = s["own"]

    def pair(j):
        nonlocal last
        s = state[j]
        s["sib"] = sibling(now(s["own"]))
        last = s["sib"]

    def send(j):
        nonlocal last
        s = state[j]
        s["own"], s["sib"] = now(s["own"], s["sib"])
        s["xs"], s["dys"], s["dest"], s["prob"], a3, b3, a1, b2 = partials(
            send_kernel, info, s["own"], s["sib"], weights, (), n_dp
        )
        s["a3"], s["b3"] = swap(a3, 1), swap(b3, 2)
        s["a1"], s["b2"] = a1, b2
        last = s["dest"]

    def keep(j):
        nonlocal last
        s = state[j]
        o, i = now(s["own"], s["sib"])
        s["xs2"], s["dys2"], s["keep"], s["weight"] = partials(
            keep_kernel, info, o, i, weights, (s["dest"], s["prob"]), n_dp
        )
        last = s["weight"]

    def sums(j):
        nonlocal last
        s = state[j]
        got_a, got_b = now(s["a3"], s["b3"])
        to_x, to_y = second(s["keep"], got_a, got_b, s["a1"], s["b2"])
        s["to_x"], s["to_y"] = swap(to_x, 1), swap(to_y, 2)
        last = to_x

    def middle(j):
        nonlocal last
        s = state[j]
        got_x, got_y = now(s["to_x"], s["to_y"])
        s["act"], s["line"] = inner(s["keep"], got_x, got_y, s["weight"], s["dest"])
        s["x"], s["y"] = swap(s["act"], 1), swap(s["act"], 2)
        last = s["act"]

    def far(j):
        nonlocal last
        s = state[j]
        s["x"], s["y"] = now(s["x"], s["y"])
        a, b = s["y"][:rows], s["x"][rows:]
        s["far_a"], s["far_b"] = swap(a, 1), swap(b, 2)
        last = (a, b)

    def back(j):
        nonlocal home, ring, last
        s = state[j]
        far_a, far_b = now(s["far_a"], s["far_b"])
        s["acts"] = (s["act"], s["x"], s["y"], far_a, far_b)
        dx_own, dx_sib = dx_chunk(info, *s["acts"], s["dest"], gate_w, up_w, s["line"], 2 * n_exp)
        last = dx_own
        dx = dx_own + sibling(dx_sib).astype(F32)
        if j == 0:
            home = dx
        else:
            if ring is not None:
                dx = dx + ring.astype(F32)
            ring = plane(dx.astype(BF16))

    state[0]["own"] = own
    pair(0)
    state[1]["came"] = plane(after(own, last))
    send(0)
    keep(0)
    sums(0)
    take(1)
    middle(0)
    pair(1)
    send(1)
    keep(1)
    far(0)
    sums(1)
    take(2)
    pair(2)
    send(2)
    keep(2)
    middle(1)
    back(0)
    for j in range(2, n_chunk):
        if j + 1 < n_chunk:
            take(j + 1)
            pair(j + 1)
        sums(j)
        far(j - 1)
        if j + 1 < n_chunk:
            send(j + 1)
            keep(j + 1)
        middle(j)
        back(j - 1)
    far(n_chunk - 1)
    back(n_chunk - 1)

    acts = [a for s in state for a in s["acts"]]
    xs = [s[k] for s in state for k in ("xs", "xs2")]
    dys = [s[k] for s in state for k in ("dys", "dys2")]
    grad_gate, grad_up = grads(info, xs, acts, [gate_w.shape, up_w.shape])
    home = (home + ring.astype(F32)).astype(BF16)
    pieces = [home[:, o * tok : (o + 1) * tok] for o in range(n_dp)]
    pieces = [pieces[0]] + [swap(pieces[o], o) for o in range(1, n_dp)]
    (grad_down,) = grads(info, dys, acts, [down_w.shape])
    grad_tokens, flat = join(info, pieces, 2 * n_exp)
    flat = flat.astype(BF16)
    by_slot = flat.reshape(n_dp, n_exp, 2, tok).transpose(1, 0, 2, 3).reshape(n_exp * local, tok)
    match = routes[:, :, None] == slot_expert[None, None, :]
    grad_probs = jnp.sum(jnp.where(match, by_slot.T[:, None, :], jnp.zeros((), BF16)), axis=2)
    return (grad_tokens, grad_probs, grad_gate, grad_up, grad_down)


def forward_part(got_x, w_gate, w_up):
    gate = jnp.einsum("sekd,edf->sekf", got_x, w_gate, preferred_element_type=jnp.float32)
    upval = jnp.einsum("sekd,edf->sekf", got_x, w_up, preferred_element_type=jnp.float32)
    sig = jax.nn.sigmoid(gate)
    act = gate * sig
    hidden = (act * upval).astype(jnp.bfloat16)
    return (gate, upval, sig, act, hidden)


def shards_weights(tokens, cotangent, routes, probs, slot_expert, gate_w, up_w, down_w):
    n_exp = lax.axis_size("expert")
    local = gate_w.shape[0]
    tok_rows = tokens.shape[0]
    top = routes.shape[1]
    width = tokens.shape[1]
    count = local * n_exp
    rows_all = count * CAP
    flat = routes.reshape(-1)
    labels = jnp.arange(count, dtype=jnp.int32)
    match = slot_expert[None, :] == labels[:, None]
    slot_of = jnp.sum(jnp.where(match, labels[None, :], 0), axis=1)
    picked = flat[:, None] == labels[None, :]
    target = jnp.sum(jnp.where(picked, slot_of[None, :], 0), axis=1)
    hits = picked.astype(jnp.int32)
    position = jnp.sum((jnp.cumsum(hits, axis=0) - hits) * hits, axis=1)
    where_row = target * CAP + position
    placed = where_row[None, :] == jnp.arange(rows_all, dtype=jnp.int32)[:, None]
    token_map = jnp.any(placed.reshape(rows_all, tok_rows, top), axis=2).astype(jnp.bfloat16)
    send_x = jnp.dot(token_map, tokens, preferred_element_type=jnp.float32).astype(jnp.bfloat16)
    send_x = send_x.reshape(n_exp, local * CAP, width)
    send_dy = jnp.dot(token_map, cotangent, preferred_element_type=jnp.float32).astype(jnp.bfloat16)
    send_dy = send_dy.reshape(n_exp, local * CAP, width)
    zero_p = jnp.zeros((), jnp.bfloat16)
    send_p = jnp.sum(jnp.where(placed, probs.reshape(-1)[None, :], zero_p), axis=1).reshape(
        n_exp, local * CAP
    )
    w_gate, w_up, w_down = (
        lax.all_gather(gate_w, "dp", axis=1, tiled=True),
        lax.all_gather(up_w, "dp", axis=1, tiled=True),
        lax.all_gather(down_w, "dp", axis=2, tiled=True),
    )
    shape_rows = (n_exp, local, CAP, width)
    got_x = lax.all_to_all(send_x, "expert", split_axis=0, concat_axis=0, tiled=True).reshape(
        shape_rows
    )
    gate, upval, sig, act, hidden = forward_part(got_x, w_gate, w_up)
    got_dy, got_p = (
        lax.all_to_all(send_dy, "expert", split_axis=0, concat_axis=0, tiled=True),
        lax.all_to_all(send_p, "expert", split_axis=0, concat_axis=0, tiled=True),
    )
    got_dy = got_dy.reshape(shape_rows)
    weight = got_p.reshape(n_exp, local, CAP).astype(jnp.float32)[..., None]
    back = jnp.einsum("sekd,efd->sekf", got_dy, w_down, preferred_element_type=jnp.float32)
    dprob = jnp.sum(hidden.astype(jnp.float32) * back, axis=-1).astype(jnp.bfloat16)
    dh = weight * back
    d_gate = (dh * upval * sig * (1.0 + gate * (1.0 - sig))).astype(jnp.bfloat16)
    d_up = (dh * act).astype(jnp.bfloat16)
    dx_rows = (
        jnp.einsum("sekf,edf->sekd", d_gate, w_gate, preferred_element_type=jnp.float32)
        + jnp.einsum("sekf,edf->sekd", d_up, w_up, preferred_element_type=jnp.float32)
    ).astype(jnp.bfloat16)
    back_x, back_p = (
        lax.all_to_all(
            dx_rows.reshape(n_exp, local * CAP, width),
            "expert",
            split_axis=0,
            concat_axis=0,
            tiled=True,
        ),
        lax.all_to_all(
            dprob.reshape(n_exp, local * CAP), "expert", split_axis=0, concat_axis=0, tiled=True
        ),
    )
    wdy = (weight * got_dy.astype(jnp.float32)).astype(jnp.bfloat16)
    part_gate = jnp.einsum("sekd,sekf->edf", got_x, d_gate, preferred_element_type=jnp.float32)
    part_up = jnp.einsum("sekd,sekf->edf", got_x, d_up, preferred_element_type=jnp.float32)
    part_down = jnp.einsum("sekf,sekd->efd", hidden, wdy, preferred_element_type=jnp.float32)
    grad_gate, grad_up, grad_down = (
        lax.psum_scatter(part_gate, "dp", scatter_dimension=1, tiled=True),
        lax.psum_scatter(part_up, "dp", scatter_dimension=1, tiled=True),
        lax.psum_scatter(part_down, "dp", scatter_dimension=2, tiled=True),
    )
    returned_rows = back_x.reshape(rows_all, width)
    grad_tokens = lax.dot_general(
        token_map, returned_rows, (((0,), (0,)), ((), ())), preferred_element_type=jnp.float32
    ).astype(jnp.bfloat16)
    grad_probs = jnp.sum(jnp.where(placed, back_p.reshape(rows_all)[:, None], zero_p), axis=0)
    grad_probs = grad_probs.reshape(tok_rows, top)
    return (grad_tokens, grad_probs, grad_gate, grad_up, grad_down)


def solution(mesh):
    placed = (
        P(("dp", "expert"), None),
        P(("dp", "expert"), None),
        P(("dp", "expert"), None),
        P(("dp", "expert"), None),
        P(),
        P("expert", "dp", None),
        P("expert", "dp", None),
        P("expert", None, "dp"),
    )
    n_dp, n_exp = mesh.shape["dp"], mesh.shape["expert"]

    def shards(*args):
        local, rows = args[5].shape[0], 2 * n_dp * CAP
        by_rows = n_dp == 4 and local == 2 * n_dp and n_exp % 2 == 0 and n_exp >= 6 and rows % 16 == 0
        return (shards_rows if by_rows else shards_weights)(*args)

    return jax.shard_map(
        shards,
        mesh=mesh,
        in_specs=placed,
        out_specs=(
            P(("dp", "expert"), None),
            P(("dp", "expert"), None),
            P("expert", "dp", None),
            P("expert", "dp", None),
            P("expert", None, "dp"),
        ),
        check_vma=False,
    )
```

```python
import functools

import jax
import jax.numpy as jnp
from jax import lax
from jax.experimental import pallas as pl
from jax.experimental.pallas import tpu as pltpu
from jax.sharding import PartitionSpec as P

CAP = 18
F32 = jnp.float32
BF16 = jnp.bfloat16
VMEM_LIMIT = 20 * 1024 * 1024
PARTIALS_LIMIT = 36 * 1024 * 1024
GRADS_LIMIT = 56 * 1024 * 1024
NT = (((1,), (1,)), ((), ()))
TN = (((0,), (0,)), ((), ()))
NN = (((1,), (0,)), ((), ()))
IN_SMEM = pl.BlockSpec(memory_space=pltpu.SMEM)
IN_VMEM = pl.BlockSpec(memory_space=pltpu.VMEM)
IN_HBM = pl.BlockSpec(memory_space=pltpu.HBM)


def mm(a, b, dims=NN):
    return lax.dot_general(a, b, dims, preferred_element_type=F32)


def params(limit=VMEM_LIMIT):
    return pltpu.CompilerParams(vmem_limit_bytes=limit)


def cost(flops, nbytes):
    return pl.CostEstimate(flops=int(flops) // 1000, bytes_accessed=int(nbytes) // 1000, transcendentals=0)


def call(body, args, token, **options):
    n = len(args)
    smem = options.pop("smem", 0)
    specs = [IN_SMEM if k < smem else IN_VMEM for k in range(n)]

    def kernel(*refs):
        body(*refs[:n], *refs[n + 1 :])

    return pl.pallas_call(
        kernel,
        in_specs=specs + [pl.BlockSpec(memory_space=pl.ANY)],
        compiler_params=params(options.pop("limit", VMEM_LIMIT)),
        **options,
    )(*args, token)


def gate_on(array, token):
    spec = pl.BlockSpec(memory_space=pl.ANY)
    return pl.pallas_call(
        lambda *refs: None,
        in_specs=[spec, spec],
        out_specs=spec,
        out_shape=jax.ShapeDtypeStruct(array.shape, array.dtype),
        input_output_aliases={0: 0},
        compiler_params=params(),
        name="gate_on",
    )(array, token)


def payload_kernel(info, tok, cot, routes, probs, experts, *outs):
    n = info[8]
    rows, width = tok.shape
    wide = width // len(outs)
    lanes = experts.shape[1]
    lane = lax.broadcasted_iota(jnp.int32, (rows, lanes), 1)
    hit = jnp.zeros((rows, lanes), F32)
    val = jnp.zeros((rows, lanes), F32)
    want = experts[...]
    rt = routes[...]
    pr = probs[...].astype(F32)
    for k in range(routes.shape[1]):
        eq = rt[:, k : k + 1] == want
        hit = jnp.where(eq, 1.0, hit)
        val = jnp.where(eq, pr[:, k : k + 1], val)
    before = (
        lax.broadcasted_iota(jnp.int32, (rows, rows), 1)
        < lax.broadcasted_iota(jnp.int32, (rows, rows), 0)
    ).astype(F32).astype(BF16)
    pos = mm(before, hit.astype(BF16))
    pos = jnp.where(hit > 0.5, pos, -1.0)
    meta = jnp.where(lane < lanes // 2, pos, val).astype(BF16)
    for o, out in enumerate(outs):
        at = pl.multiple_of((n ^ o) * wide, wide)
        out[:, :wide] = tok[:, pl.ds(at, wide)]
        out[:, wide : 2 * wide] = cot[:, pl.ds(at, wide)]
        out[:, 2 * wide :] = meta


def payload(info, tokens, cotangent, routes, probs, slot_expert, n_dp):
    rows, width = tokens.shape
    wide = width // n_dp
    twice = jnp.concatenate([slot_expert, slot_expert])[None, :]
    cols = 2 * wide + twice.shape[1]
    return pl.pallas_call(
        payload_kernel,
        in_specs=[pl.BlockSpec(memory_space=pltpu.SMEM)] + [pl.BlockSpec(memory_space=pltpu.VMEM)] * 5,
        out_specs=[pl.BlockSpec(memory_space=pltpu.VMEM)] * n_dp,
        out_shape=[jax.ShapeDtypeStruct((rows, cols), BF16)] * n_dp,
        compiler_params=params(),
        name="payload",
    )(info, tokens, cotangent, routes, probs, twice)


def ready_kernel(gate, up, down, out):
    out[...] = (gate[0, :16, :128] + up[0, :16, :128] + down[0, :16, :128]).astype(F32)


def ready(weights, token):
    return call(
        ready_kernel,
        list(weights),
        token,
        out_specs=IN_VMEM,
        out_shape=jax.ShapeDtypeStruct((16, 128), F32),
        cost_estimate=cost(1, 1000),
        name="ready",
    )


def stack_kernel(*refs):
    out = refs[-1]
    rows = refs[0].shape[0]
    for k, ref in enumerate(refs[:-1]):
        out[k * rows : (k + 1) * rows, :] = ref[...]


def stack(pieces, token):
    rows, cols = pieces[0].shape
    return call(
        stack_kernel,
        pieces,
        token,
        out_specs=IN_VMEM,
        out_shape=jax.ShapeDtypeStruct((rows * len(pieces), cols), BF16),
        cost_estimate=cost(1, 1000),
        name="stack",
    )


def some_slots(info, base, own, sib, gate, up, down, dest, xs_out, dys_out, pick, xs, dys, sems, put):
    rows, wide = xs.shape[1:]
    m = own.shape[0]
    for q in range(4):
        hot = lax.broadcasted_iota(jnp.int32, (rows, 2 * m), 0) == dest[base + q]
        pick[q * rows : (q + 1) * rows, :] = hot.astype(F32).astype(BF16)
    for k, buf in enumerate((xs, dys)):
        at = slice(k * wide, (k + 1) * wide)
        part = mm(pick[:, :m], own[:, at]) + mm(pick[:, m:], sib[:, at])
        for q in range(4):
            buf[q] = part[q * rows : (q + 1) * rows].astype(BF16)
    copies = [
        pltpu.make_async_copy(xs, xs_out, sems.at[0]),
        pltpu.make_async_copy(dys, dys_out, sems.at[1]),
    ]
    for copy in copies:
        copy.start()
    for q in range(4):
        slot = info[base + q]
        put(q, 0, mm(xs[q], gate[slot]))
        put(q, 1, mm(xs[q], up[slot]))
        put(q, 2, mm(dys[q], down[slot], NT))
    for copy in copies:
        copy.wait()


def send_kernel(n_dp, info, own, sib, gate, up, down, *refs):
    xs_out, dys_out, dest, prob, a3, b3, a1, b2, scr, pick, xs, dys, sems = refs
    n, first, core = info[8], info[9], info[10]
    wide = xs.shape[-1]
    half = scr.shape[1] // 2
    tok = own.shape[0] // n_dp
    f = gate.shape[2]
    for c, src in enumerate((own, sib)):
        for o in range(n_dp):
            scr[c * n_dp + o] = src[o * tok : (o + 1) * tok, 2 * wide :].astype(F32).T
    for q in range(8):
        row = first + info[q]
        for c in range(2):
            for o in range(n_dp):
                k = c * n_dp + o
                at = slice(k * tok, (k + 1) * tok)
                pos = scr[k, pl.ds(row, 1), :]
                off = (((n ^ o) * 2 + (core ^ c)) * CAP).astype(F32)
                dest[q, :, at] = jnp.where(pos < 0, -1.0, pos + off).astype(jnp.int32)
                if q >= 6:
                    prob[q - 6, :, at] = scr[k, pl.ds(half + row, 1), :]

    def put(q, part, value):
        (a3, b3, a1, b2)[q][:, part * f : (part + 1) * f] = value.astype(BF16)

    some_slots(info, 0, own, sib, gate, up, down, dest, xs_out, dys_out, pick, xs, dys, sems, put)


def keep_kernel(n_dp, info, own, sib, gate, up, down, dest, prob, *refs):
    xs_out, dys_out, keep, weight, pick, xs, dys, sems = refs
    f = gate.shape[2]

    def put(q, part, value):
        keep[q, :, part * f : (part + 1) * f] = value

    for h in range(2):
        hot = lax.broadcasted_iota(jnp.int32, (keep.shape[1], dest.shape[2]), 0) == dest[6 + h]
        p = jnp.sum(jnp.where(hot, prob[h], 0.0), axis=1, keepdims=True)
        weight[h] = jnp.broadcast_to(p, weight.shape[1:])
    some_slots(info, 4, own, sib, gate, up, down, dest, xs_out, dys_out, pick, xs, dys, sems, put)


def partials(kernel, info, own, sib, weights, small, n_dp, token):
    wide, f = weights[0].shape[1:]
    rows = 2 * n_dp * CAP
    m = own.shape[0]
    args = [info, own, sib, *weights, *small]
    out_shape = [jax.ShapeDtypeStruct((4, rows, wide), BF16)] * 2
    scratch = [pltpu.VMEM((4 * rows, 2 * m), BF16)]
    scratch += [pltpu.VMEM((4, rows, wide), BF16)] * 2 + [pltpu.SemaphoreType.DMA((2,))]
    if small:
        out_shape += [jax.ShapeDtypeStruct((4, rows, 3 * f), F32), jax.ShapeDtypeStruct((2, rows, 128), F32)]
    else:
        out_shape += [jax.ShapeDtypeStruct((8, 1, 2 * m), jnp.int32), jax.ShapeDtypeStruct((2, 1, 2 * m), F32)]
        out_shape += [jax.ShapeDtypeStruct((rows, 3 * f), BF16)] * 4
        scratch = [pltpu.VMEM((2 * n_dp, own.shape[1] - 2 * wide, m // n_dp), F32)] + scratch
    return call(
        functools.partial(kernel, n_dp),
        args,
        token,
        smem=1,
        limit=PARTIALS_LIMIT,
        out_specs=[IN_HBM] * 2 + [IN_VMEM] * (len(out_shape) - 2),
        scratch_shapes=scratch,
        out_shape=out_shape,
        cost_estimate=cost(8 * rows * (2 * m * 2 * wide + wide * 3 * f), 8e6),
        name="partials_keep" if small else "partials_send",
    )


def sums_kernel(keep, got_a, got_b, raw_a, raw_b, to_x, to_y):
    to_x[0] = raw_a[...]
    to_x[1] = (keep[1] + got_b[...].astype(F32)).astype(BF16)
    to_y[0] = (keep[0] + got_a[...].astype(F32)).astype(BF16)
    to_y[1] = raw_b[...]


def second(keep, got_a, got_b, raw_a, raw_b, token):
    return call(
        sums_kernel,
        [keep, got_a, got_b, raw_a, raw_b],
        token,
        out_specs=[IN_VMEM] * 2,
        out_shape=[jax.ShapeDtypeStruct((2,) + raw_a.shape, BF16)] * 2,
        cost_estimate=cost(2 * raw_a.size, 4e6),
        name="sums",
    )


def far_kernel(from_x, from_y, out_a, out_b):
    rows = out_a.shape[0]
    out_a[...] = from_y[:rows, :]
    out_b[...] = from_x[rows:, :]


def far_rows(from_x, from_y, token):
    shape = jax.ShapeDtypeStruct((from_x.shape[0] // 2, from_x.shape[1]), BF16)
    return call(
        far_kernel,
        [from_x, from_y],
        token,
        out_specs=[IN_VMEM] * 2,
        out_shape=[shape] * 2,
        cost_estimate=cost(from_x.size, 4e6),
        name="far_rows",
    )


def inner_kernel(keep, got_x, got_y, prob, dest, act, line):
    f = act.shape[1] // 3
    rows = keep.shape[1]
    for h in range(2):
        t = keep[2 + h] + got_x[h].astype(F32) + got_y[h].astype(F32)
        g, u, r = t[:, :f], t[:, f : 2 * f], t[:, 2 * f :]
        sg = jax.nn.sigmoid(g)
        silu = g * sg
        hid = silu * u
        p = prob[h][:, :1]
        pr = p * r
        hb = hid.astype(BF16).astype(F32)
        dprob = jnp.sum(hb * r, axis=1, keepdims=True)
        at = slice(h * rows, (h + 1) * rows)
        act[at, :f] = (pr * u * sg * (1.0 + g * (1.0 - sg))).astype(BF16)
        act[at, f : 2 * f] = (pr * silu).astype(BF16)
        act[at, 2 * f :] = (p * hid).astype(BF16)
        want = dest[6 + h]
        eq = lax.broadcasted_iota(jnp.int32, (rows, want.shape[1]), 0) == want
        line[pl.ds(h, 1), :] = jnp.sum(jnp.where(eq, dprob, 0.0), axis=0, keepdims=True)


def inner(keep, got_x, got_y, prob, dest, token):
    rows, f3 = keep.shape[1:]
    return call(
        inner_kernel,
        [keep, got_x, got_y, prob, dest],
        token,
        out_specs=[IN_VMEM] * 2,
        out_shape=[
            jax.ShapeDtypeStruct((2 * rows, f3), BF16),
            jax.ShapeDtypeStruct((2, dest.shape[2]), F32),
        ],
        cost_estimate=cost(2 * rows * f3 * 20, 6e6),
        name="inner",
    )


def in_order(own, from_x, from_y, far_a, far_b):
    rows = far_a.shape[0]
    return [
        (far_a, 0),
        (far_b, 0),
        (from_x, 0),
        (from_y, rows),
        (from_y, 0),
        (from_x, rows),
        (own, 0),
        (own, rows),
    ]


def dx_kernel(info, own, from_x, from_y, far_a, far_b, dest, gate, up, line, out_own, out_sib, hot_s, dx_s):
    rows = far_a.shape[0]
    f = gate.shape[2]
    m = out_own.shape[1]
    pieces = in_order(own, from_x, from_y, far_a, far_b)
    for q, (ref, lo) in enumerate(pieces):
        a = ref[lo : lo + rows, : 2 * f]
        at = slice(q * rows, (q + 1) * rows)
        back = mm(a[:, :f], gate[info[q]], NT) + mm(a[:, f:], up[info[q]], NT)
        dx_s[at, :] = back.astype(BF16)
        hot = lax.broadcasted_iota(jnp.int32, (rows, 2 * m), 0) == dest[q]
        hot_s[at, :] = hot.astype(F32).astype(BF16)
    wide = dx_s.shape[1]
    extra = out_own.shape[0] - wide
    row = lax.broadcasted_iota(jnp.int32, (extra, 2 * m), 0) - 2 * info[11]
    lines = jnp.where(row == 0, line[0:1, :], jnp.where(row == 1, line[1:2, :], 0.0))
    for c, out in enumerate((out_own, out_sib)):
        at = slice(c * m, (c + 1) * m)
        out[:wide, :] = mm(dx_s[...], hot_s[:, at], TN).astype(out.dtype)
        out[wide:, :] = lines[:, at].astype(out.dtype)


def dx_chunk(info, own, from_x, from_y, far_a, far_b, dest, gate_w, up_w, line, extra, token):
    wide, f = gate_w.shape[1:]
    rows = far_a.shape[0]
    total = dest.shape[-1]
    return call(
        dx_kernel,
        [info, own, from_x, from_y, far_a, far_b, dest, gate_w, up_w, line],
        token,
        smem=1,
        out_specs=[IN_VMEM, IN_VMEM],
        scratch_shapes=[pltpu.VMEM((8 * rows, total), BF16), pltpu.VMEM((8 * rows, wide), BF16)],
        out_shape=[
            jax.ShapeDtypeStruct((wide + extra, total // 2), F32),
            jax.ShapeDtypeStruct((wide + extra, total // 2), BF16),
        ],
        cost_estimate=cost(2 * 8 * rows * (2 * f * wide + total * wide), 12e6),
        name="dx",
    )


def grads_kernel(n_chunk, is_in, info, *refs):
    halves, acts = refs[: 2 * n_chunk], refs[2 * n_chunk : 7 * n_chunk]
    n_out = 2 if is_in else 1
    outs = refs[7 * n_chunk : 7 * n_chunk + n_out]
    row_s, act_s, out_s, in_sems, out_sems = refs[7 * n_chunk + n_out :]
    rows = row_s.shape[1] // n_chunk
    cols = act_s.shape[2]
    f = cols // n_out
    col = pl.ds(0 if is_in else 2 * f, cols)

    def loads(q):
        out = []
        for k in range(n_chunk):
            at = pl.ds(k * rows, rows)
            ref, lo = in_order(*acts[5 * k : 5 * k + 5])[q]
            src = halves[2 * k + q // 4].at[q % 4]
            out.append(pltpu.make_async_copy(src, row_s.at[q % 2, at], in_sems.at[q % 2, 2 * k]))
            src = ref.at[pl.ds(lo, rows), col]
            out.append(pltpu.make_async_copy(src, act_s.at[q % 2, at], in_sems.at[q % 2, 2 * k + 1]))
        return out

    def stores(q):
        return [
            pltpu.make_async_copy(out_s.at[q % 2, k], outs[k].at[info[q]], out_sems.at[q % 2, k])
            for k in range(n_out)
        ]

    for copy in loads(0):
        copy.start()
    for q in range(8):
        if q < 7:
            for copy in loads(q + 1):
                copy.start()
        for copy in loads(q):
            copy.wait()
        if q >= 2:
            for copy in stores(q - 2):
                copy.wait()
        if is_in:
            both = mm(row_s[q % 2], act_s[q % 2], TN)
            out_s[q % 2, 0] = both[:, :f]
            out_s[q % 2, 1] = both[:, f:]
        else:
            out_s[q % 2, 0] = mm(act_s[q % 2], row_s[q % 2], TN)
        for copy in stores(q):
            copy.start()
    for q in (6, 7):
        for copy in stores(q):
            copy.wait()


def grads(info, halves, acts, shapes):
    n_chunk = len(halves) // 2
    is_in = len(shapes) == 2
    rows, wide = halves[0].shape[1:]
    cols = acts[0].shape[1] // 3 * len(shapes)
    any_spec = pl.BlockSpec(memory_space=pl.ANY)
    return pl.pallas_call(
        functools.partial(grads_kernel, n_chunk, is_in),
        in_specs=[IN_SMEM] + [any_spec] * (7 * n_chunk),
        out_specs=[any_spec] * len(shapes),
        scratch_shapes=[
            pltpu.VMEM((2, n_chunk * rows, wide), BF16),
            pltpu.VMEM((2, n_chunk * rows, cols), BF16),
            pltpu.VMEM((2, len(shapes)) + shapes[0][1:], F32),
            pltpu.SemaphoreType.DMA((2, 2 * n_chunk)),
            pltpu.SemaphoreType.DMA((2, len(shapes))),
        ],
        out_shape=[jax.ShapeDtypeStruct(s, F32) for s in shapes],
        compiler_params=params(GRADS_LIMIT),
        cost_estimate=cost(1000 * 16 * n_chunk * rows * wide * cols, 2e10),
        name="grads_in" if is_in else "grads_out",
    )(info, *halves, *acts)


def join_kernel(info, *refs):
    out, table = refs[-2:]
    wide = out.shape[1] // (len(refs) - 2)
    for o, piece in enumerate(refs[:-2]):
        at = pl.ds(pl.multiple_of((info[8] ^ o) * wide, wide), wide)
        out[:, at] = piece[:wide, :].astype(F32).T.astype(BF16)
        table[info[8] ^ o] = piece[wide:, :].astype(F32)


def join(info, pieces, extra):
    wide, rows = pieces[0].shape[0] - extra, pieces[0].shape[1]
    return pl.pallas_call(
        join_kernel,
        in_specs=[IN_SMEM] + [IN_VMEM] * len(pieces),
        out_specs=[IN_VMEM] * 2,
        out_shape=[
            jax.ShapeDtypeStruct((rows, wide * len(pieces)), BF16),
            jax.ShapeDtypeStruct((len(pieces), extra, rows), F32),
        ],
        compiler_params=params(),
        name="join",
    )(info, *pieces)


def shards_rows(tokens, cotangent, routes, probs, slot_expert, gate_w, up_w, down_w):
    n_dp, n_exp = lax.axis_size("dp"), lax.axis_size("expert")
    local = gate_w.shape[0]
    tok = tokens.shape[0]
    n_chunk = n_exp // 2
    rows = 2 * n_dp * CAP
    n, e = lax.axis_index("dp"), lax.axis_index("expert")
    order = [3, 7, 1, 6, 2, 5, 0, 4]
    info = jnp.stack(
        [2 * (n ^ (k % 4)) + k // 4 for k in order]
        + [n, e * local, e % 2, e]
    ).astype(jnp.int32)

    def swap(a, o):
        return lax.ppermute(a, "dp", [(k, k ^ o) for k in range(n_dp)])

    def sibling(a):
        return lax.ppermute(a, "expert", [(k, k ^ 1) for k in range(n_exp)])

    def after(a, b):
        return lax.optimization_barrier((a, b))[0]

    def plane(a):
        return lax.ppermute(a, "expert", [(k, (k + 2) % n_exp) for k in range(n_exp)])

    last = info
    weights = (gate_w, up_w, down_w)
    sends = payload(info, tokens, cotangent, routes, probs, slot_expert, n_dp)
    pieces = [sends[0]] + [swap(sends[o], o) for o in range(1, n_dp)]
    own = stack(pieces, ready(weights, sends[0]))
    home, ring = None, None
    state = [dict() for _ in range(n_chunk)]

    def take(j):
        nonlocal last
        s = state[j]
        s["own"] = last = gate_on(s["came"], last)
        if j + 1 < n_chunk:
            state[j + 1]["came"] = plane(s["own"])

    def pair(j):
        state[j]["sib"] = sibling(state[j]["own"])

    def send(j):
        nonlocal last
        s = state[j]
        s["xs"], s["dys"], s["dest"], s["prob"], a3, b3, s["a1"], s["b2"] = partials(
            send_kernel, info, s["own"], s["sib"], weights, (), n_dp, last
        )
        s["a3"], s["b3"] = swap(a3, 1), swap(b3, 2)
        last = s["dest"]

    def keep(j):
        nonlocal last
        s = state[j]
        s["xs2"], s["dys2"], s["keep"], s["weight"] = partials(
            keep_kernel, info, s["own"], s["sib"], weights, (s["dest"], s["prob"]), n_dp, last
        )
        last = s["weight"]

    def sums(j):
        nonlocal last
        s = state[j]
        to_x, to_y = second(s["keep"], s["a3"], s["b3"], s["a1"], s["b2"], last)
        s["to_x"], s["to_y"] = swap(to_x, 1), swap(to_y, 2)
        last = to_x

    def middle(j):
        nonlocal last
        s = state[j]
        s["act"], s["line"] = inner(s["keep"], s["to_x"], s["to_y"], s["weight"], s["dest"], last)
        s["x"], s["y"] = swap(s["act"], 1), swap(s["act"], 2)
        last = s["line"]

    def far(j):
        nonlocal last
        s = state[j]
        a, b = far_rows(s["x"], s["y"], last)
        s["far_a"], s["far_b"] = swap(a, 1), swap(b, 2)
        last = a

    def back(j):
        nonlocal home, ring, last
        s = state[j]
        s["acts"] = (s["act"], s["x"], s["y"], s["far_a"], s["far_b"])
        dx_own, dx_sib = dx_chunk(info, *s["acts"], s["dest"], gate_w, up_w, s["line"], 2 * n_exp, last)
        last = dx_own
        dx = dx_own + sibling(dx_sib).astype(F32)
        if j == 0:
            home = dx
        else:
            if ring is not None:
                dx = dx + ring.astype(F32)
            ring = plane(dx.astype(BF16))

    state[0]["own"] = own
    pair(0)
    state[1]["came"] = plane(after(own, state[0]["sib"]))
    send(0)
    keep(0)
    sums(0)
    middle(0)
    take(1)
    pair(1)
    send(1)
    keep(1)
    far(0)
    sums(1)
    take(2)
    pair(2)
    send(2)
    keep(2)
    middle(1)
    back(0)
    for j in range(2, n_chunk):
        sums(j)
        far(j - 1)
        if j + 1 < n_chunk:
            take(j + 1)
            pair(j + 1)
            send(j + 1)
            keep(j + 1)
        middle(j)
        back(j - 1)
    far(n_chunk - 1)
    back(n_chunk - 1)

    acts = [a for s in state for a in s["acts"]]
    xs = [s[k] for s in state for k in ("xs", "xs2")]
    dys = [s[k] for s in state for k in ("dys", "dys2")]
    grad_gate, grad_up = grads(info, xs, acts, [gate_w.shape, up_w.shape])
    home = (home + ring.astype(F32)).astype(BF16)
    pieces = [home[:, o * tok : (o + 1) * tok] for o in range(n_dp)]
    pieces = [pieces[0]] + [swap(pieces[o], o) for o in range(1, n_dp)]
    (grad_down,) = grads(info, dys, acts, [down_w.shape])
    grad_tokens, flat = join(info, pieces, 2 * n_exp)
    flat = flat.astype(BF16)
    by_slot = flat.reshape(n_dp, n_exp, 2, tok).transpose(1, 0, 2, 3).reshape(n_exp * local, tok)
    match = routes[:, :, None] == slot_expert[None, None, :]
    grad_probs = jnp.sum(jnp.where(match, by_slot.T[:, None, :], jnp.zeros((), BF16)), axis=2)
    return (grad_tokens, grad_probs, grad_gate, grad_up, grad_down)


def forward_part(got_x, w_gate, w_up):
    gate = jnp.einsum("sekd,edf->sekf", got_x, w_gate, preferred_element_type=jnp.float32)
    upval = jnp.einsum("sekd,edf->sekf", got_x, w_up, preferred_element_type=jnp.float32)
    sig = jax.nn.sigmoid(gate)
    act = gate * sig
    hidden = (act * upval).astype(jnp.bfloat16)
    return (gate, upval, sig, act, hidden)


def shards_weights(tokens, cotangent, routes, probs, slot_expert, gate_w, up_w, down_w):
    n_exp = lax.axis_size("expert")
    local = gate_w.shape[0]
    tok_rows = tokens.shape[0]
    top = routes.shape[1]
    width = tokens.shape[1]
    count = local * n_exp
    rows_all = count * CAP
    flat = routes.reshape(-1)
    labels = jnp.arange(count, dtype=jnp.int32)
    match = slot_expert[None, :] == labels[:, None]
    slot_of = jnp.sum(jnp.where(match, labels[None, :], 0), axis=1)
    picked = flat[:, None] == labels[None, :]
    target = jnp.sum(jnp.where(picked, slot_of[None, :], 0), axis=1)
    hits = picked.astype(jnp.int32)
    position = jnp.sum((jnp.cumsum(hits, axis=0) - hits) * hits, axis=1)
    where_row = target * CAP + position
    placed = where_row[None, :] == jnp.arange(rows_all, dtype=jnp.int32)[:, None]
    token_map = jnp.any(placed.reshape(rows_all, tok_rows, top), axis=2).astype(jnp.bfloat16)
    send_x = jnp.dot(token_map, tokens, preferred_element_type=jnp.float32).astype(jnp.bfloat16)
    send_x = send_x.reshape(n_exp, local * CAP, width)
    send_dy = jnp.dot(token_map, cotangent, preferred_element_type=jnp.float32).astype(jnp.bfloat16)
    send_dy = send_dy.reshape(n_exp, local * CAP, width)
    zero_p = jnp.zeros((), jnp.bfloat16)
    send_p = jnp.sum(jnp.where(placed, probs.reshape(-1)[None, :], zero_p), axis=1).reshape(
        n_exp, local * CAP
    )
    w_gate, w_up, w_down = (
        lax.all_gather(gate_w, "dp", axis=1, tiled=True),
        lax.all_gather(up_w, "dp", axis=1, tiled=True),
        lax.all_gather(down_w, "dp", axis=2, tiled=True),
    )
    shape_rows = (n_exp, local, CAP, width)
    got_x = lax.all_to_all(send_x, "expert", split_axis=0, concat_axis=0, tiled=True).reshape(
        shape_rows
    )
    gate, upval, sig, act, hidden = forward_part(got_x, w_gate, w_up)
    got_dy, got_p = (
        lax.all_to_all(send_dy, "expert", split_axis=0, concat_axis=0, tiled=True),
        lax.all_to_all(send_p, "expert", split_axis=0, concat_axis=0, tiled=True),
    )
    got_dy = got_dy.reshape(shape_rows)
    weight = got_p.reshape(n_exp, local, CAP).astype(jnp.float32)[..., None]
    back = jnp.einsum("sekd,efd->sekf", got_dy, w_down, preferred_element_type=jnp.float32)
    dprob = jnp.sum(hidden.astype(jnp.float32) * back, axis=-1).astype(jnp.bfloat16)
    dh = weight * back
    d_gate = (dh * upval * sig * (1.0 + gate * (1.0 - sig))).astype(jnp.bfloat16)
    d_up = (dh * act).astype(jnp.bfloat16)
    dx_rows = (
        jnp.einsum("sekf,edf->sekd", d_gate, w_gate, preferred_element_type=jnp.float32)
        + jnp.einsum("sekf,edf->sekd", d_up, w_up, preferred_element_type=jnp.float32)
    ).astype(jnp.bfloat16)
    back_x, back_p = (
        lax.all_to_all(
            dx_rows.reshape(n_exp, local * CAP, width),
            "expert",
            split_axis=0,
            concat_axis=0,
            tiled=True,
        ),
        lax.all_to_all(
            dprob.reshape(n_exp, local * CAP), "expert", split_axis=0, concat_axis=0, tiled=True
        ),
    )
    wdy = (weight * got_dy.astype(jnp.float32)).astype(jnp.bfloat16)
    part_gate = jnp.einsum("sekd,sekf->edf", got_x, d_gate, preferred_element_type=jnp.float32)
    part_up = jnp.einsum("sekd,sekf->edf", got_x, d_up, preferred_element_type=jnp.float32)
    part_down = jnp.einsum("sekf,sekd->efd", hidden, wdy, preferred_element_type=jnp.float32)
    grad_gate, grad_up, grad_down = (
        lax.psum_scatter(part_gate, "dp", scatter_dimension=1, tiled=True),
        lax.psum_scatter(part_up, "dp", scatter_dimension=1, tiled=True),
        lax.psum_scatter(part_down, "dp", scatter_dimension=2, tiled=True),
    )
    returned_rows = back_x.reshape(rows_all, width)
    grad_tokens = lax.dot_general(
        token_map, returned_rows, (((0,), (0,)), ((), ())), preferred_element_type=jnp.float32
    ).astype(jnp.bfloat16)
    grad_probs = jnp.sum(jnp.where(placed, back_p.reshape(rows_all)[:, None], zero_p), axis=0)
    grad_probs = grad_probs.reshape(tok_rows, top)
    return (grad_tokens, grad_probs, grad_gate, grad_up, grad_down)


def solution(mesh):
    placed = (
        P(("dp", "expert"), None),
        P(("dp", "expert"), None),
        P(("dp", "expert"), None),
        P(("dp", "expert"), None),
        P(),
        P("expert", "dp", None),
        P("expert", "dp", None),
        P("expert", None, "dp"),
    )
    n_dp, n_exp = mesh.shape["dp"], mesh.shape["expert"]

    def shards(*args):
        local, rows = args[5].shape[0], 2 * n_dp * CAP
        by_rows = n_dp == 4 and local == 2 * n_dp and n_exp % 2 == 0 and n_exp >= 6 and rows % 16 == 0
        return (shards_rows if by_rows else shards_weights)(*args)

    return jax.shard_map(
        shards,
        mesh=mesh,
        in_specs=placed,
        out_specs=(
            P(("dp", "expert"), None),
            P(("dp", "expert"), None),
            P("expert", "dp", None),
            P("expert", "dp", None),
            P("expert", None, "dp"),
        ),
        check_vma=False,
    )
```

```python
import functools

import jax
import jax.numpy as jnp
from jax import lax
from jax.experimental import pallas as pl
from jax.experimental.pallas import tpu as pltpu
from jax.sharding import PartitionSpec as P

CAP = 18
F32 = jnp.float32
BF16 = jnp.bfloat16
VMEM_LIMIT = 20 * 1024 * 1024
PARTIALS_LIMIT = 36 * 1024 * 1024
GRADS_LIMIT = 56 * 1024 * 1024
NT = (((1,), (1,)), ((), ()))
TN = (((0,), (0,)), ((), ()))
NN = (((1,), (0,)), ((), ()))
IN_SMEM = pl.BlockSpec(memory_space=pltpu.SMEM)
IN_VMEM = pl.BlockSpec(memory_space=pltpu.VMEM)
IN_HBM = pl.BlockSpec(memory_space=pltpu.HBM)


def mm(a, b, dims=NN):
    return lax.dot_general(a, b, dims, preferred_element_type=F32)


def params(limit=VMEM_LIMIT):
    return pltpu.CompilerParams(vmem_limit_bytes=limit)


def cost(flops, nbytes):
    return pl.CostEstimate(flops=int(flops) // 1000, bytes_accessed=int(nbytes) // 1000, transcendentals=0)


def call(body, args, token, **options):
    n = len(args)
    smem = options.pop("smem", 0)
    specs = [IN_SMEM if k < smem else IN_VMEM for k in range(n)]

    def kernel(*refs):
        body(*refs[:n], *refs[n + 1 :])

    return pl.pallas_call(
        kernel,
        in_specs=specs + [pl.BlockSpec(memory_space=pl.ANY)],
        compiler_params=params(options.pop("limit", VMEM_LIMIT)),
        **options,
    )(*args, token)


def gate_on(array, token):
    spec = pl.BlockSpec(memory_space=pl.ANY)
    return pl.pallas_call(
        lambda *refs: None,
        in_specs=[spec, spec],
        out_specs=spec,
        out_shape=jax.ShapeDtypeStruct(array.shape, array.dtype),
        input_output_aliases={0: 0},
        compiler_params=params(),
        name="gate_on",
    )(array, token)


def payload_kernel(n_dp, info, *refs):
    outs, (tok, cot, routes, probs, experts, twice, sems) = refs[5 : 5 + n_dp], refs[5 + n_dp :]
    copies = [
        pltpu.make_async_copy(src, dst, sems.at[k])
        for k, (src, dst) in enumerate(zip(refs[:5], (tok, cot, routes, probs, experts)))
    ]
    for copy in copies:
        copy.start()
    for copy in copies[2:]:
        copy.wait()
    n = info[8]
    rows, width = tok.shape
    wide = width // n_dp
    lanes = twice.shape[1]
    twice[:, : lanes // 2] = experts[...]
    twice[:, lanes // 2 :] = experts[...]
    lane = lax.broadcasted_iota(jnp.int32, (rows, lanes), 1)
    hit = jnp.zeros((rows, lanes), F32)
    val = jnp.zeros((rows, lanes), F32)
    want = twice[...].astype(F32)
    rt = routes[...].astype(F32).T
    pr = probs[...].astype(F32).T
    for k in range(routes.shape[0]):
        eq = rt[:, k : k + 1] == want
        hit = jnp.where(eq, 1.0, hit)
        val = jnp.where(eq, pr[:, k : k + 1], val)
    before = (
        lax.broadcasted_iota(jnp.int32, (rows, rows), 1)
        < lax.broadcasted_iota(jnp.int32, (rows, rows), 0)
    ).astype(F32).astype(BF16)
    pos = mm(before, hit.astype(BF16))
    pos = jnp.where(hit > 0.5, pos, -1.0)
    meta = jnp.where(lane < lanes // 2, pos, val).astype(BF16)
    for copy in copies[:2]:
        copy.wait()
    for o, out in enumerate(outs):
        at = pl.multiple_of((n ^ o) * wide, wide)
        out[:, :wide] = tok[:, pl.ds(at, wide)]
        out[:, wide : 2 * wide] = cot[:, pl.ds(at, wide)]
        out[:, 2 * wide :] = meta


def payload(info, tokens, cotangent, routes, probs, slot_expert, n_dp):
    rows, width = tokens.shape
    lanes = 2 * slot_expert.shape[0]
    cols = 2 * (width // n_dp) + lanes
    args = [tokens, cotangent, routes.T, probs.T, slot_expert[None, :]]
    return pl.pallas_call(
        functools.partial(payload_kernel, n_dp),
        in_specs=[IN_SMEM] + [pl.BlockSpec(memory_space=pl.ANY)] * 5,
        out_specs=[IN_VMEM] * n_dp,
        out_shape=[jax.ShapeDtypeStruct((rows, cols), BF16)] * n_dp,
        scratch_shapes=[pltpu.VMEM(a.shape, a.dtype) for a in args]
        + [pltpu.VMEM((1, lanes), jnp.int32), pltpu.SemaphoreType.DMA((5,))],
        compiler_params=params(GRADS_LIMIT),
        name="payload",
    )(info, *args)


def ready_kernel(gate, up, down, out):
    out[...] = (gate[0, :16, :128] + up[0, :16, :128] + down[0, :16, :128]).astype(F32)


def ready(weights, token):
    return call(
        ready_kernel,
        list(weights),
        token,
        out_specs=IN_VMEM,
        out_shape=jax.ShapeDtypeStruct((16, 128), F32),
        cost_estimate=cost(1, 1000),
        name="ready",
    )


def stack_kernel(*refs):
    out = refs[-1]
    rows = refs[0].shape[0]
    for k, ref in enumerate(refs[:-1]):
        out[k * rows : (k + 1) * rows, :] = ref[...]


def stack(pieces, token):
    rows, cols = pieces[0].shape
    return call(
        stack_kernel,
        pieces,
        token,
        out_specs=IN_VMEM,
        out_shape=jax.ShapeDtypeStruct((rows * len(pieces), cols), BF16),
        cost_estimate=cost(1, 1000),
        name="stack",
    )


def some_slots(info, base, own, sib, gate, up, down, dest, rows_out, pick, got, sem, put):
    rows, wide = got.shape[1], got.shape[2] // 2
    m = own.shape[0]
    for q in range(4):
        hot = lax.broadcasted_iota(jnp.int32, (rows, 2 * m), 0) == dest[base + q]
        pick[q * rows : (q + 1) * rows, :] = hot.astype(F32).astype(BF16)
    for k in range(2):
        at = slice(k * wide, (k + 1) * wide)
        part = mm(pick[:, :m], own[:, at]) + mm(pick[:, m:], sib[:, at])
        for q in range(4):
            got[q, :, at] = part[q * rows : (q + 1) * rows].astype(BF16)
    copy = pltpu.make_async_copy(got, rows_out, sem)
    copy.start()
    for q in range(4):
        slot = info[base + q]
        x, dy = got[q, :, :wide], got[q, :, wide:]
        put(q, 0, mm(x, gate[slot]))
        put(q, 1, mm(x, up[slot]))
        put(q, 2, mm(dy, down[slot], NT))
    copy.wait()


def send_kernel(n_dp, info, own, sib, gate, up, down, *refs):
    rows_out, dest, prob, a3, b3, a1, b2, scr, pick, got, sem = refs
    n, first, core = info[8], info[9], info[10]
    wide = rows_out.shape[-1] // 2
    half = scr.shape[1] // 2
    tok = own.shape[0] // n_dp
    f = gate.shape[2]
    for c, src in enumerate((own, sib)):
        for o in range(n_dp):
            scr[c * n_dp + o] = src[o * tok : (o + 1) * tok, 2 * wide :].astype(F32).T
    for q in range(8):
        row = first + info[q]
        for c in range(2):
            for o in range(n_dp):
                k = c * n_dp + o
                at = slice(k * tok, (k + 1) * tok)
                pos = scr[k, pl.ds(row, 1), :]
                off = (((n ^ o) * 2 + (core ^ c)) * CAP).astype(F32)
                dest[q, :, at] = jnp.where(pos < 0, -1.0, pos + off).astype(jnp.int32)
                if q >= 6:
                    prob[q - 6, :, at] = scr[k, pl.ds(half + row, 1), :]

    def put(q, part, value):
        (a3, b3, a1, b2)[q][:, part * f : (part + 1) * f] = value.astype(BF16)

    some_slots(info, 0, own, sib, gate, up, down, dest, rows_out, pick, got, sem, put)


def keep_kernel(n_dp, info, own, sib, gate, up, down, dest, prob, *refs):
    rows_out, keep, weight, pick, got, sem = refs
    f = gate.shape[2]

    def put(q, part, value):
        keep[q, :, part * f : (part + 1) * f] = value

    for h in range(2):
        hot = lax.broadcasted_iota(jnp.int32, (keep.shape[1], dest.shape[2]), 0) == dest[6 + h]
        p = jnp.sum(jnp.where(hot, prob[h], 0.0), axis=1, keepdims=True)
        weight[h] = jnp.broadcast_to(p, weight.shape[1:])
    some_slots(info, 4, own, sib, gate, up, down, dest, rows_out, pick, got, sem, put)


def partials(kernel, info, own, sib, weights, small, n_dp, token):
    wide, f = weights[0].shape[1:]
    rows = 2 * n_dp * CAP
    m = own.shape[0]
    args = [info, own, sib, *weights, *small]
    out_shape = [jax.ShapeDtypeStruct((4, rows, 2 * wide), BF16)]
    scratch = [pltpu.VMEM((4 * rows, 2 * m), BF16)]
    scratch += [pltpu.VMEM((4, rows, 2 * wide), BF16), pltpu.SemaphoreType.DMA]
    if small:
        out_shape += [jax.ShapeDtypeStruct((4, rows, 3 * f), F32), jax.ShapeDtypeStruct((2, rows, 128), F32)]
    else:
        out_shape += [jax.ShapeDtypeStruct((8, 1, 2 * m), jnp.int32), jax.ShapeDtypeStruct((2, 1, 2 * m), F32)]
        out_shape += [jax.ShapeDtypeStruct((rows, 3 * f), BF16)] * 4
        scratch = [pltpu.VMEM((2 * n_dp, own.shape[1] - 2 * wide, m // n_dp), F32)] + scratch
    return call(
        functools.partial(kernel, n_dp),
        args,
        token,
        smem=1,
        limit=PARTIALS_LIMIT,
        out_specs=[IN_HBM] + [IN_VMEM] * (len(out_shape) - 1),
        scratch_shapes=scratch,
        out_shape=out_shape,
        cost_estimate=cost(8 * rows * (2 * m * 2 * wide + wide * 3 * f), 8e6),
        name="partials_keep" if small else "partials_send",
    )


def sums_kernel(keep, got_a, got_b, raw_a, raw_b, to_x, to_y):
    to_x[0] = raw_a[...]
    to_x[1] = (keep[1] + got_b[...].astype(F32)).astype(BF16)
    to_y[0] = (keep[0] + got_a[...].astype(F32)).astype(BF16)
    to_y[1] = raw_b[...]


def second(keep, got_a, got_b, raw_a, raw_b, token):
    return call(
        sums_kernel,
        [keep, got_a, got_b, raw_a, raw_b],
        token,
        out_specs=[IN_VMEM] * 2,
        out_shape=[jax.ShapeDtypeStruct((2,) + raw_a.shape, BF16)] * 2,
        cost_estimate=cost(2 * raw_a.size, 4e6),
        name="sums",
    )


def far_kernel(from_x, from_y, out_a, out_b):
    rows = out_a.shape[0]
    out_a[...] = from_y[:rows, :]
    out_b[...] = from_x[rows:, :]


def far_rows(from_x, from_y, token):
    shape = jax.ShapeDtypeStruct((from_x.shape[0] // 2, from_x.shape[1]), BF16)
    return call(
        far_kernel,
        [from_x, from_y],
        token,
        out_specs=[IN_VMEM] * 2,
        out_shape=[shape] * 2,
        cost_estimate=cost(from_x.size, 4e6),
        name="far_rows",
    )


def inner_kernel(keep, got_x, got_y, prob, dest, act, line):
    f = act.shape[1] // 3
    rows = keep.shape[1]
    for h in range(2):
        t = keep[2 + h] + got_x[h].astype(F32) + got_y[h].astype(F32)
        g, u, r = t[:, :f], t[:, f : 2 * f], t[:, 2 * f :]
        sg = jax.nn.sigmoid(g)
        silu = g * sg
        hid = silu * u
        p = prob[h][:, :1]
        pr = p * r
        hb = hid.astype(BF16).astype(F32)
        dprob = jnp.sum(hb * r, axis=1, keepdims=True)
        at = slice(h * rows, (h + 1) * rows)
        act[at, :f] = (pr * u * sg * (1.0 + g * (1.0 - sg))).astype(BF16)
        act[at, f : 2 * f] = (pr * silu).astype(BF16)
        act[at, 2 * f :] = (p * hid).astype(BF16)
        want = dest[6 + h]
        eq = lax.broadcasted_iota(jnp.int32, (rows, want.shape[1]), 0) == want
        line[pl.ds(h, 1), :] = jnp.sum(jnp.where(eq, dprob, 0.0), axis=0, keepdims=True)


def inner(keep, got_x, got_y, prob, dest, token):
    rows, f3 = keep.shape[1:]
    return call(
        inner_kernel,
        [keep, got_x, got_y, prob, dest],
        token,
        out_specs=[IN_VMEM] * 2,
        out_shape=[
            jax.ShapeDtypeStruct((2 * rows, f3), BF16),
            jax.ShapeDtypeStruct((2, dest.shape[2]), F32),
        ],
        cost_estimate=cost(2 * rows * f3 * 20, 6e6),
        name="inner",
    )


def in_order(own, from_x, from_y, far_a, far_b):
    rows = far_a.shape[0]
    return [
        (far_a, 0),
        (far_b, 0),
        (from_x, 0),
        (from_y, rows),
        (from_y, 0),
        (from_x, rows),
        (own, 0),
        (own, rows),
    ]


def dx_kernel(info, own, from_x, from_y, far_a, far_b, dest, gate, up, line, out_own, out_sib, hot_s, dx_s):
    rows = far_a.shape[0]
    f = gate.shape[2]
    m = out_own.shape[1]
    pieces = in_order(own, from_x, from_y, far_a, far_b)
    for q, (ref, lo) in enumerate(pieces):
        a = ref[lo : lo + rows, : 2 * f]
        at = slice(q * rows, (q + 1) * rows)
        back = mm(a[:, :f], gate[info[q]], NT) + mm(a[:, f:], up[info[q]], NT)
        dx_s[at, :] = back.astype(BF16)
        hot = lax.broadcasted_iota(jnp.int32, (rows, 2 * m), 0) == dest[q]
        hot_s[at, :] = hot.astype(F32).astype(BF16)
    wide = dx_s.shape[1]
    extra = out_own.shape[0] - wide
    row = lax.broadcasted_iota(jnp.int32, (extra, 2 * m), 0) - 2 * info[11]
    lines = jnp.where(row == 0, line[0:1, :], jnp.where(row == 1, line[1:2, :], 0.0))
    for c, out in enumerate((out_own, out_sib)):
        at = slice(c * m, (c + 1) * m)
        out[:wide, :] = mm(dx_s[...], hot_s[:, at], TN).astype(out.dtype)
        out[wide:, :] = lines[:, at].astype(out.dtype)


def dx_chunk(info, own, from_x, from_y, far_a, far_b, dest, gate_w, up_w, line, extra, token):
    wide, f = gate_w.shape[1:]
    rows = far_a.shape[0]
    total = dest.shape[-1]
    return call(
        dx_kernel,
        [info, own, from_x, from_y, far_a, far_b, dest, gate_w, up_w, line],
        token,
        smem=1,
        out_specs=[IN_VMEM, IN_VMEM],
        scratch_shapes=[pltpu.VMEM((8 * rows, total), BF16), pltpu.VMEM((8 * rows, wide), BF16)],
        out_shape=[
            jax.ShapeDtypeStruct((wide + extra, total // 2), F32),
            jax.ShapeDtypeStruct((wide + extra, total // 2), BF16),
        ],
        cost_estimate=cost(2 * 8 * rows * (2 * f * wide + total * wide), 12e6),
        name="dx",
    )


def grads_kernel(n_chunk, is_in, info, *refs):
    halves, acts = refs[: 2 * n_chunk], refs[2 * n_chunk : 7 * n_chunk]
    n_out = 2 if is_in else 1
    outs = refs[7 * n_chunk : 7 * n_chunk + n_out]
    row_s, act_s, out_s, in_sems, out_sems = refs[7 * n_chunk + n_out :]
    rows = row_s.shape[1] // n_chunk
    cols = act_s.shape[2]
    f = cols // n_out
    col = pl.ds(0 if is_in else 2 * f, cols)
    wide = row_s.shape[2]
    half = pl.ds(0 if is_in else wide, wide)

    def loads(q):
        out = []
        for k in range(n_chunk):
            at = pl.ds(k * rows, rows)
            ref, lo = in_order(*acts[5 * k : 5 * k + 5])[q]
            src = halves[2 * k + q // 4].at[q % 4, :, half]
            out.append(pltpu.make_async_copy(src, row_s.at[q % 2, at], in_sems.at[q % 2, 2 * k]))
            src = ref.at[pl.ds(lo, rows), col]
            out.append(pltpu.make_async_copy(src, act_s.at[q % 2, at], in_sems.at[q % 2, 2 * k + 1]))
        return out

    def stores(q):
        return [
            pltpu.make_async_copy(out_s.at[q % 2, k], outs[k].at[info[q]], out_sems.at[q % 2, k])
            for k in range(n_out)
        ]

    for copy in loads(0):
        copy.start()
    for q in range(8):
        if q < 7:
            for copy in loads(q + 1):
                copy.start()
        for copy in loads(q):
            copy.wait()
        if q >= 2:
            for copy in stores(q - 2):
                copy.wait()
        if is_in:
            both = mm(row_s[q % 2], act_s[q % 2], TN)
            out_s[q % 2, 0] = both[:, :f]
            out_s[q % 2, 1] = both[:, f:]
        else:
            out_s[q % 2, 0] = mm(act_s[q % 2], row_s[q % 2], TN)
        for copy in stores(q):
            copy.start()
    for q in (6, 7):
        for copy in stores(q):
            copy.wait()


def grads(info, halves, acts, shapes):
    n_chunk = len(halves) // 2
    is_in = len(shapes) == 2
    rows, wide = halves[0].shape[1], halves[0].shape[2] // 2
    cols = acts[0].shape[1] // 3 * len(shapes)
    any_spec = pl.BlockSpec(memory_space=pl.ANY)
    return pl.pallas_call(
        functools.partial(grads_kernel, n_chunk, is_in),
        in_specs=[IN_SMEM] + [any_spec] * (7 * n_chunk),
        out_specs=[any_spec] * len(shapes),
        scratch_shapes=[
            pltpu.VMEM((2, n_chunk * rows, wide), BF16),
            pltpu.VMEM((2, n_chunk * rows, cols), BF16),
            pltpu.VMEM((2, len(shapes)) + shapes[0][1:], F32),
            pltpu.SemaphoreType.DMA((2, 2 * n_chunk)),
            pltpu.SemaphoreType.DMA((2, len(shapes))),
        ],
        out_shape=[jax.ShapeDtypeStruct(s, F32) for s in shapes],
        compiler_params=params(GRADS_LIMIT),
        cost_estimate=cost(1000 * 16 * n_chunk * rows * wide * cols, 2e10),
        name="grads_in" if is_in else "grads_out",
    )(info, *halves, *acts)


def join_kernel(info, routes, experts, *refs):
    out, probs, table = refs[-3:]
    pieces = refs[:-3]
    wide = out.shape[1] // len(pieces)
    extra = pieces[0].shape[0] - wide
    for o, piece in enumerate(pieces):
        at = pl.ds(pl.multiple_of((info[8] ^ o) * wide, wide), wide)
        out[:, at] = piece[:wide, :].astype(F32).T.astype(BF16)
        at = pl.ds(pl.multiple_of((info[8] ^ o) * extra, extra), extra)
        table[at, :] = piece[wide:, :].astype(F32)
    found = table[...].T
    rt = routes[...].astype(F32).T
    want = experts[...].astype(F32)
    for k in range(rt.shape[1]):
        hit = jnp.where(rt[:, k : k + 1] == want, found, 0.0)
        probs[:, k : k + 1] = jnp.sum(hit, axis=1, keepdims=True).astype(BF16)


def join(info, routes, experts, pieces, extra):
    wide, rows = pieces[0].shape[0] - extra, pieces[0].shape[1]
    return pl.pallas_call(
        join_kernel,
        in_specs=[IN_SMEM] + [IN_VMEM] * (2 + len(pieces)),
        out_specs=[IN_VMEM] * 2,
        out_shape=[
            jax.ShapeDtypeStruct((rows, wide * len(pieces)), BF16),
            jax.ShapeDtypeStruct(routes.shape[::-1], BF16),
        ],
        scratch_shapes=[pltpu.VMEM((extra * len(pieces), rows), F32)],
        compiler_params=params(),
        name="join",
    )(info, routes, experts, *pieces)


def shards_rows(tokens, cotangent, routes, probs, slot_expert, gate_w, up_w, down_w):
    n_dp, n_exp = lax.axis_size("dp"), lax.axis_size("expert")
    local = gate_w.shape[0]
    tok = tokens.shape[0]
    n_chunk = n_exp // 2
    rows = 2 * n_dp * CAP
    n, e = lax.axis_index("dp"), lax.axis_index("expert")
    order = [3, 7, 1, 6, 2, 5, 0, 4]
    info = jnp.stack(
        [2 * (n ^ (k % 4)) + k // 4 for k in order]
        + [n, e * local, e % 2, e]
    ).astype(jnp.int32)

    def swap(a, o):
        return lax.ppermute(a, "dp", [(k, k ^ o) for k in range(n_dp)])

    def sibling(a):
        return lax.ppermute(a, "expert", [(k, k ^ 1) for k in range(n_exp)])

    def after(a, b):
        return lax.optimization_barrier((a, b))[0]

    def plane(a):
        return lax.ppermute(a, "expert", [(k, (k + 2) % n_exp) for k in range(n_exp)])

    last = info
    weights = (gate_w, up_w, down_w)
    sends = payload(info, tokens, cotangent, routes, probs, slot_expert, n_dp)
    pieces = [sends[0]] + [swap(sends[o], o) for o in range(1, n_dp)]
    own = stack(pieces, ready(weights, sends[0]))
    home, ring = None, None
    state = [dict() for _ in range(n_chunk)]

    def take(j):
        nonlocal last
        s = state[j]
        s["own"] = last = gate_on(s["came"], last)
        if j + 1 < n_chunk:
            state[j + 1]["came"] = plane(s["own"])

    def pair(j):
        state[j]["sib"] = sibling(state[j]["own"])

    def send(j):
        nonlocal last
        s = state[j]
        s["rows"], s["dest"], s["prob"], a3, b3, s["a1"], s["b2"] = partials(
            send_kernel, info, s["own"], s["sib"], weights, (), n_dp, last
        )
        s["a3"], s["b3"] = swap(a3, 1), swap(b3, 2)
        last = s["dest"]

    def keep(j):
        nonlocal last
        s = state[j]
        s["rows2"], s["keep"], s["weight"] = partials(
            keep_kernel, info, s["own"], s["sib"], weights, (s["dest"], s["prob"]), n_dp, last
        )
        last = s["weight"]

    def sums(j):
        nonlocal last
        s = state[j]
        to_x, to_y = second(s["keep"], s["a3"], s["b3"], s["a1"], s["b2"], last)
        s["to_x"], s["to_y"] = swap(to_x, 1), swap(to_y, 2)
        last = to_x

    def middle(j):
        nonlocal last
        s = state[j]
        s["act"], s["line"] = inner(s["keep"], s["to_x"], s["to_y"], s["weight"], s["dest"], last)
        s["x"], s["y"] = swap(s["act"], 1), swap(s["act"], 2)
        last = s["line"]

    def far(j):
        nonlocal last
        s = state[j]
        a, b = far_rows(s["x"], s["y"], last)
        s["far_a"], s["far_b"] = swap(a, 1), swap(b, 2)
        last = a

    def back(j):
        nonlocal home, ring, last
        s = state[j]
        s["acts"] = (s["act"], s["x"], s["y"], s["far_a"], s["far_b"])
        dx_own, dx_sib = dx_chunk(info, *s["acts"], s["dest"], gate_w, up_w, s["line"], 2 * n_exp, last)
        last = dx_own
        dx = dx_own + sibling(dx_sib).astype(F32)
        if j == 0:
            home = dx
        else:
            if ring is not None:
                dx = dx + ring.astype(F32)
            ring = plane(dx.astype(BF16))

    state[0]["own"] = own
    pair(0)
    state[1]["came"] = plane(after(own, state[0]["sib"]))
    send(0)
    keep(0)
    sums(0)
    middle(0)
    take(1)
    pair(1)
    send(1)
    keep(1)
    far(0)
    sums(1)
    take(2)
    pair(2)
    send(2)
    keep(2)
    middle(1)
    back(0)
    for j in range(2, n_chunk):
        sums(j)
        far(j - 1)
        if j + 1 < n_chunk:
            take(j + 1)
            pair(j + 1)
            send(j + 1)
            keep(j + 1)
        middle(j)
        back(j - 1)
    far(n_chunk - 1)
    back(n_chunk - 1)

    acts = [a for s in state for a in s["acts"]]
    got = [s[k] for s in state for k in ("rows", "rows2")]
    grad_gate, grad_up = grads(info, got, acts, [gate_w.shape, up_w.shape])
    home = (home + ring.astype(F32)).astype(BF16)
    pieces = [home[:, o * tok : (o + 1) * tok] for o in range(n_dp)]
    pieces = [pieces[0]] + [swap(pieces[o], o) for o in range(1, n_dp)]
    (grad_down,) = grads(info, got, acts, [down_w.shape])
    experts = slot_expert.reshape(n_exp, n_dp, 2).transpose(1, 0, 2).reshape(1, -1)
    grad_tokens, grad_probs = join(info, routes.T, experts, pieces, 2 * n_exp)
    return (grad_tokens, grad_probs, grad_gate, grad_up, grad_down)


def forward_part(got_x, w_gate, w_up):
    gate = jnp.einsum("sekd,edf->sekf", got_x, w_gate, preferred_element_type=jnp.float32)
    upval = jnp.einsum("sekd,edf->sekf", got_x, w_up, preferred_element_type=jnp.float32)
    sig = jax.nn.sigmoid(gate)
    act = gate * sig
    hidden = (act * upval).astype(jnp.bfloat16)
    return (gate, upval, sig, act, hidden)


def shards_weights(tokens, cotangent, routes, probs, slot_expert, gate_w, up_w, down_w):
    n_exp = lax.axis_size("expert")
    local = gate_w.shape[0]
    tok_rows = tokens.shape[0]
    top = routes.shape[1]
    width = tokens.shape[1]
    count = local * n_exp
    rows_all = count * CAP
    flat = routes.reshape(-1)
    labels = jnp.arange(count, dtype=jnp.int32)
    match = slot_expert[None, :] == labels[:, None]
    slot_of = jnp.sum(jnp.where(match, labels[None, :], 0), axis=1)
    picked = flat[:, None] == labels[None, :]
    target = jnp.sum(jnp.where(picked, slot_of[None, :], 0), axis=1)
    hits = picked.astype(jnp.int32)
    position = jnp.sum((jnp.cumsum(hits, axis=0) - hits) * hits, axis=1)
    where_row = target * CAP + position
    placed = where_row[None, :] == jnp.arange(rows_all, dtype=jnp.int32)[:, None]
    token_map = jnp.any(placed.reshape(rows_all, tok_rows, top), axis=2).astype(jnp.bfloat16)
    send_x = jnp.dot(token_map, tokens, preferred_element_type=jnp.float32).astype(jnp.bfloat16)
    send_x = send_x.reshape(n_exp, local * CAP, width)
    send_dy = jnp.dot(token_map, cotangent, preferred_element_type=jnp.float32).astype(jnp.bfloat16)
    send_dy = send_dy.reshape(n_exp, local * CAP, width)
    zero_p = jnp.zeros((), jnp.bfloat16)
    send_p = jnp.sum(jnp.where(placed, probs.reshape(-1)[None, :], zero_p), axis=1).reshape(
        n_exp, local * CAP
    )
    w_gate, w_up, w_down = (
        lax.all_gather(gate_w, "dp", axis=1, tiled=True),
        lax.all_gather(up_w, "dp", axis=1, tiled=True),
        lax.all_gather(down_w, "dp", axis=2, tiled=True),
    )
    shape_rows = (n_exp, local, CAP, width)
    got_x = lax.all_to_all(send_x, "expert", split_axis=0, concat_axis=0, tiled=True).reshape(
        shape_rows
    )
    gate, upval, sig, act, hidden = forward_part(got_x, w_gate, w_up)
    got_dy, got_p = (
        lax.all_to_all(send_dy, "expert", split_axis=0, concat_axis=0, tiled=True),
        lax.all_to_all(send_p, "expert", split_axis=0, concat_axis=0, tiled=True),
    )
    got_dy = got_dy.reshape(shape_rows)
    weight = got_p.reshape(n_exp, local, CAP).astype(jnp.float32)[..., None]
    back = jnp.einsum("sekd,efd->sekf", got_dy, w_down, preferred_element_type=jnp.float32)
    dprob = jnp.sum(hidden.astype(jnp.float32) * back, axis=-1).astype(jnp.bfloat16)
    dh = weight * back
    d_gate = (dh * upval * sig * (1.0 + gate * (1.0 - sig))).astype(jnp.bfloat16)
    d_up = (dh * act).astype(jnp.bfloat16)
    dx_rows = (
        jnp.einsum("sekf,edf->sekd", d_gate, w_gate, preferred_element_type=jnp.float32)
        + jnp.einsum("sekf,edf->sekd", d_up, w_up, preferred_element_type=jnp.float32)
    ).astype(jnp.bfloat16)
    back_x, back_p = (
        lax.all_to_all(
            dx_rows.reshape(n_exp, local * CAP, width),
            "expert",
            split_axis=0,
            concat_axis=0,
            tiled=True,
        ),
        lax.all_to_all(
            dprob.reshape(n_exp, local * CAP), "expert", split_axis=0, concat_axis=0, tiled=True
        ),
    )
    wdy = (weight * got_dy.astype(jnp.float32)).astype(jnp.bfloat16)
    part_gate = jnp.einsum("sekd,sekf->edf", got_x, d_gate, preferred_element_type=jnp.float32)
    part_up = jnp.einsum("sekd,sekf->edf", got_x, d_up, preferred_element_type=jnp.float32)
    part_down = jnp.einsum("sekf,sekd->efd", hidden, wdy, preferred_element_type=jnp.float32)
    grad_gate, grad_up, grad_down = (
        lax.psum_scatter(part_gate, "dp", scatter_dimension=1, tiled=True),
        lax.psum_scatter(part_up, "dp", scatter_dimension=1, tiled=True),
        lax.psum_scatter(part_down, "dp", scatter_dimension=2, tiled=True),
    )
    returned_rows = back_x.reshape(rows_all, width)
    grad_tokens = lax.dot_general(
        token_map, returned_rows, (((0,), (0,)), ((), ())), preferred_element_type=jnp.float32
    ).astype(jnp.bfloat16)
    grad_probs = jnp.sum(jnp.where(placed, back_p.reshape(rows_all)[:, None], zero_p), axis=0)
    grad_probs = grad_probs.reshape(tok_rows, top)
    return (grad_tokens, grad_probs, grad_gate, grad_up, grad_down)


def solution(mesh):
    placed = (
        P(("dp", "expert"), None),
        P(("dp", "expert"), None),
        P(("dp", "expert"), None),
        P(("dp", "expert"), None),
        P(),
        P("expert", "dp", None),
        P("expert", "dp", None),
        P("expert", None, "dp"),
    )
    n_dp, n_exp = mesh.shape["dp"], mesh.shape["expert"]

    def shards(*args):
        local, rows = args[5].shape[0], 2 * n_dp * CAP
        by_rows = n_dp == 4 and local == 2 * n_dp and n_exp % 2 == 0 and n_exp >= 6 and rows % 16 == 0
        return (shards_rows if by_rows else shards_weights)(*args)

    return jax.shard_map(
        shards,
        mesh=mesh,
        in_specs=placed,
        out_specs=(
            P(("dp", "expert"), None),
            P(("dp", "expert"), None),
            P("expert", "dp", None),
            P("expert", "dp", None),
            P("expert", None, "dp"),
        ),
        check_vma=False,
    )
```

```python
import functools

import jax
import jax.numpy as jnp
from jax import lax
from jax.experimental import pallas as pl
from jax.experimental.pallas import tpu as pltpu
from jax.sharding import PartitionSpec as P

CAP = 18
F32 = jnp.float32
BF16 = jnp.bfloat16
VMEM_LIMIT = 20 * 1024 * 1024
PARTIALS_LIMIT = 36 * 1024 * 1024
GRADS_LIMIT = 56 * 1024 * 1024
NT = (((1,), (1,)), ((), ()))
TN = (((0,), (0,)), ((), ()))
NN = (((1,), (0,)), ((), ()))
IN_SMEM = pl.BlockSpec(memory_space=pltpu.SMEM)
IN_VMEM = pl.BlockSpec(memory_space=pltpu.VMEM)
IN_HBM = pl.BlockSpec(memory_space=pltpu.HBM)


def mm(a, b, dims=NN):
    return lax.dot_general(a, b, dims, preferred_element_type=F32)


def params(limit=VMEM_LIMIT):
    return pltpu.CompilerParams(vmem_limit_bytes=limit)


def cost(flops, nbytes):
    return pl.CostEstimate(flops=int(flops) // 1000, bytes_accessed=int(nbytes) // 1000, transcendentals=0)


def call(body, args, token, **options):
    n = len(args)
    smem = options.pop("smem", 0)
    specs = [IN_SMEM if k < smem else IN_VMEM for k in range(n)]

    def kernel(*refs):
        body(*refs[:n], *refs[n + 1 :])

    return pl.pallas_call(
        kernel,
        in_specs=specs + [pl.BlockSpec(memory_space=pl.ANY)],
        compiler_params=params(options.pop("limit", VMEM_LIMIT)),
        **options,
    )(*args, token)


def gate_on(array, token):
    spec = pl.BlockSpec(memory_space=pl.ANY)
    return pl.pallas_call(
        lambda *refs: None,
        in_specs=[spec, spec],
        out_specs=spec,
        out_shape=jax.ShapeDtypeStruct(array.shape, array.dtype),
        input_output_aliases={0: 0},
        compiler_params=params(),
        name="gate_on",
    )(array, token)


def payload_kernel(n_dp, info, *refs):
    outs, (tok, cot, routes, probs, experts, twice, sems) = refs[5 : 5 + n_dp], refs[5 + n_dp :]
    copies = [
        pltpu.make_async_copy(src, dst, sems.at[k])
        for k, (src, dst) in enumerate(zip(refs[:5], (tok, cot, routes, probs, experts)))
    ]
    for copy in copies:
        copy.start()
    for copy in copies[2:]:
        copy.wait()
    n = info[8]
    rows, width = tok.shape
    wide = width // n_dp
    lanes = twice.shape[1]
    twice[:, : lanes // 2] = experts[...]
    twice[:, lanes // 2 :] = experts[...]
    lane = lax.broadcasted_iota(jnp.int32, (rows, lanes), 1)
    hit = jnp.zeros((rows, lanes), F32)
    val = jnp.zeros((rows, lanes), F32)
    want = twice[...].astype(F32)
    rt = routes[...].astype(F32).T
    pr = probs[...].astype(F32).T
    for k in range(routes.shape[0]):
        eq = rt[:, k : k + 1] == want
        hit = jnp.where(eq, 1.0, hit)
        val = jnp.where(eq, pr[:, k : k + 1], val)
    before = (
        lax.broadcasted_iota(jnp.int32, (rows, rows), 1)
        < lax.broadcasted_iota(jnp.int32, (rows, rows), 0)
    ).astype(F32).astype(BF16)
    pos = mm(before, hit.astype(BF16))
    pos = jnp.where(hit > 0.5, pos, -1.0)
    meta = jnp.where(lane < lanes // 2, pos, val).astype(BF16)
    for copy in copies[:2]:
        copy.wait()
    for o, out in enumerate(outs):
        at = pl.multiple_of((n ^ o) * wide, wide)
        out[:, :wide] = tok[:, pl.ds(at, wide)]
        out[:, wide : 2 * wide] = cot[:, pl.ds(at, wide)]
        out[:, 2 * wide :] = meta


def payload(info, tokens, cotangent, routes, probs, slot_expert, n_dp):
    rows, width = tokens.shape
    lanes = 2 * slot_expert.shape[0]
    cols = 2 * (width // n_dp) + lanes
    args = [tokens, cotangent, routes.T, probs.T, slot_expert[None, :]]
    return pl.pallas_call(
        functools.partial(payload_kernel, n_dp),
        in_specs=[IN_SMEM] + [pl.BlockSpec(memory_space=pl.ANY)] * 5,
        out_specs=[IN_VMEM] * n_dp,
        out_shape=[jax.ShapeDtypeStruct((rows, cols), BF16)] * n_dp,
        scratch_shapes=[pltpu.VMEM(a.shape, a.dtype) for a in args]
        + [pltpu.VMEM((1, lanes), jnp.int32), pltpu.SemaphoreType.DMA((5,))],
        compiler_params=params(GRADS_LIMIT),
        name="payload",
    )(info, *args)


def ready_kernel(gate, up, down, out):
    out[...] = (gate[0, :16, :128] + up[0, :16, :128] + down[0, :16, :128]).astype(F32)


def ready(weights, token):
    return call(
        ready_kernel,
        list(weights),
        token,
        out_specs=IN_VMEM,
        out_shape=jax.ShapeDtypeStruct((16, 128), F32),
        cost_estimate=cost(1, 1000),
        name="ready",
    )


def stack_kernel(*refs):
    out = refs[-1]
    rows = refs[0].shape[0]
    for k, ref in enumerate(refs[:-1]):
        out[k * rows : (k + 1) * rows, :] = ref[...]


def stack(pieces, token):
    rows, cols = pieces[0].shape
    return call(
        stack_kernel,
        pieces,
        token,
        out_specs=IN_VMEM,
        out_shape=jax.ShapeDtypeStruct((rows * len(pieces), cols), BF16),
        cost_estimate=cost(1, 1000),
        name="stack",
    )


def some_slots(info, base, own, sib, gate, up, down, dest, rows_out, pick, got, sem, put):
    rows, wide = got.shape[1], got.shape[2] // 2
    m = own.shape[0]
    for q in range(4):
        hot = lax.broadcasted_iota(jnp.int32, (rows, 2 * m), 0) == dest[base + q]
        pick[q * rows : (q + 1) * rows, :] = hot.astype(F32).astype(BF16)
    for k in range(2):
        at = slice(k * wide, (k + 1) * wide)
        part = mm(pick[:, :m], own[:, at]) + mm(pick[:, m:], sib[:, at])
        for q in range(4):
            got[q, :, at] = part[q * rows : (q + 1) * rows].astype(BF16)
    copy = pltpu.make_async_copy(got, rows_out, sem)
    copy.start()
    for q in range(4):
        slot = info[base + q]
        x, dy = got[q, :, :wide], got[q, :, wide:]
        put(q, 0, mm(x, gate[slot]))
        put(q, 1, mm(x, up[slot]))
        put(q, 2, mm(dy, down[slot], NT))
    copy.wait()


def send_kernel(n_dp, info, own, sib, gate, up, down, *refs):
    rows_out, dest, prob, a3, b3, a1, b2, scr, pick, got, sem = refs
    n, first, core = info[8], info[9], info[10]
    wide = rows_out.shape[-1] // 2
    half = scr.shape[1] // 2
    tok = own.shape[0] // n_dp
    f = gate.shape[2]
    for c, src in enumerate((own, sib)):
        for o in range(n_dp):
            scr[c * n_dp + o] = src[o * tok : (o + 1) * tok, 2 * wide :].astype(F32).T
    for q in range(8):
        row = first + info[q]
        for c in range(2):
            for o in range(n_dp):
                k = c * n_dp + o
                at = slice(k * tok, (k + 1) * tok)
                pos = scr[k, pl.ds(row, 1), :]
                off = (((n ^ o) * 2 + (core ^ c)) * CAP).astype(F32)
                dest[q, :, at] = jnp.where(pos < 0, -1.0, pos + off).astype(jnp.int32)
                if q >= 6:
                    prob[q - 6, :, at] = scr[k, pl.ds(half + row, 1), :]

    def put(q, part, value):
        (a3, b3, a1, b2)[q][:, part * f : (part + 1) * f] = value.astype(BF16)

    some_slots(info, 0, own, sib, gate, up, down, dest, rows_out, pick, got, sem, put)


def keep_kernel(n_dp, info, own, sib, gate, up, down, dest, prob, *refs):
    rows_out, keep, weight, pick, got, sem = refs
    f = gate.shape[2]

    def put(q, part, value):
        keep[q, :, part * f : (part + 1) * f] = value

    for h in range(2):
        hot = lax.broadcasted_iota(jnp.int32, (keep.shape[1], dest.shape[2]), 0) == dest[6 + h]
        p = jnp.sum(jnp.where(hot, prob[h], 0.0), axis=1, keepdims=True)
        weight[h] = jnp.broadcast_to(p, weight.shape[1:])
    some_slots(info, 4, own, sib, gate, up, down, dest, rows_out, pick, got, sem, put)


def partials(kernel, info, own, sib, weights, small, n_dp, token):
    wide, f = weights[0].shape[1:]
    rows = 2 * n_dp * CAP
    m = own.shape[0]
    args = [info, own, sib, *weights, *small]
    out_shape = [jax.ShapeDtypeStruct((4, rows, 2 * wide), BF16)]
    scratch = [pltpu.VMEM((4 * rows, 2 * m), BF16)]
    scratch += [pltpu.VMEM((4, rows, 2 * wide), BF16), pltpu.SemaphoreType.DMA]
    if small:
        out_shape += [jax.ShapeDtypeStruct((4, rows, 3 * f), F32), jax.ShapeDtypeStruct((2, rows, 128), F32)]
    else:
        out_shape += [jax.ShapeDtypeStruct((8, 1, 2 * m), jnp.int32), jax.ShapeDtypeStruct((2, 1, 2 * m), F32)]
        out_shape += [jax.ShapeDtypeStruct((rows, 3 * f), BF16)] * 4
        scratch = [pltpu.VMEM((2 * n_dp, own.shape[1] - 2 * wide, m // n_dp), F32)] + scratch
    return call(
        functools.partial(kernel, n_dp),
        args,
        token,
        smem=1,
        limit=PARTIALS_LIMIT,
        out_specs=[IN_HBM] + [IN_VMEM] * (len(out_shape) - 1),
        scratch_shapes=scratch,
        out_shape=out_shape,
        cost_estimate=cost(8 * rows * (2 * m * 2 * wide + wide * 3 * f), 8e6),
        name="partials_keep" if small else "partials_send",
    )


def sums_kernel(keep, got_a, got_b, raw_a, raw_b, to_x, to_y):
    to_x[0] = raw_a[...]
    to_x[1] = (keep[1] + got_b[...].astype(F32)).astype(BF16)
    to_y[0] = (keep[0] + got_a[...].astype(F32)).astype(BF16)
    to_y[1] = raw_b[...]


def second(keep, got_a, got_b, raw_a, raw_b, token):
    return call(
        sums_kernel,
        [keep, got_a, got_b, raw_a, raw_b],
        token,
        out_specs=[IN_VMEM] * 2,
        out_shape=[jax.ShapeDtypeStruct((2,) + raw_a.shape, BF16)] * 2,
        cost_estimate=cost(2 * raw_a.size, 4e6),
        name="sums",
    )


def far_kernel(from_x, from_y, out_a, out_b):
    rows = out_a.shape[0]
    out_a[...] = from_y[:rows, :]
    out_b[...] = from_x[rows:, :]


def far_rows(from_x, from_y, token):
    shape = jax.ShapeDtypeStruct((from_x.shape[0] // 2, from_x.shape[1]), BF16)
    return call(
        far_kernel,
        [from_x, from_y],
        token,
        out_specs=[IN_VMEM] * 2,
        out_shape=[shape] * 2,
        cost_estimate=cost(from_x.size, 4e6),
        name="far_rows",
    )


def inner_kernel(keep, got_x, got_y, prob, dest, act, line):
    f = act.shape[1] // 3
    rows = keep.shape[1]
    for h in range(2):
        t = keep[2 + h] + got_x[h].astype(F32) + got_y[h].astype(F32)
        g, u, r = t[:, :f], t[:, f : 2 * f], t[:, 2 * f :]
        sg = jax.nn.sigmoid(g)
        silu = g * sg
        hid = silu * u
        p = prob[h][:, :1]
        pr = p * r
        hb = hid.astype(BF16).astype(F32)
        dprob = jnp.sum(hb * r, axis=1, keepdims=True)
        at = slice(h * rows, (h + 1) * rows)
        act[at, :f] = (pr * u * sg * (1.0 + g * (1.0 - sg))).astype(BF16)
        act[at, f : 2 * f] = (pr * silu).astype(BF16)
        act[at, 2 * f :] = (p * hid).astype(BF16)
        want = dest[6 + h]
        eq = lax.broadcasted_iota(jnp.int32, (rows, want.shape[1]), 0) == want
        line[pl.ds(h, 1), :] = jnp.sum(jnp.where(eq, dprob, 0.0), axis=0, keepdims=True)


def inner(keep, got_x, got_y, prob, dest, token):
    rows, f3 = keep.shape[1:]
    return call(
        inner_kernel,
        [keep, got_x, got_y, prob, dest],
        token,
        out_specs=[IN_VMEM] * 2,
        out_shape=[
            jax.ShapeDtypeStruct((2 * rows, f3), BF16),
            jax.ShapeDtypeStruct((2, dest.shape[2]), F32),
        ],
        cost_estimate=cost(2 * rows * f3 * 20, 6e6),
        name="inner",
    )


def in_order(own, from_x, from_y, far_a, far_b):
    rows = far_a.shape[0]
    return [
        (far_a, 0),
        (far_b, 0),
        (from_x, 0),
        (from_y, rows),
        (from_y, 0),
        (from_x, rows),
        (own, 0),
        (own, rows),
    ]


def dx_kernel(info, own, from_x, from_y, far_a, far_b, dest, gate, up, line, out_own, out_sib, hot_s, dx_s):
    rows = far_a.shape[0]
    f = gate.shape[2]
    m = out_own.shape[1]
    pieces = in_order(own, from_x, from_y, far_a, far_b)
    for q, (ref, lo) in enumerate(pieces):
        a = ref[lo : lo + rows, : 2 * f]
        at = slice(q * rows, (q + 1) * rows)
        back = mm(a[:, :f], gate[info[q]], NT) + mm(a[:, f:], up[info[q]], NT)
        dx_s[at, :] = back.astype(BF16)
        hot = lax.broadcasted_iota(jnp.int32, (rows, 2 * m), 0) == dest[q]
        hot_s[at, :] = hot.astype(F32).astype(BF16)
    wide = dx_s.shape[1]
    extra = out_own.shape[0] - wide
    row = lax.broadcasted_iota(jnp.int32, (extra, 2 * m), 0) - 2 * info[11]
    lines = jnp.where(row == 0, line[0:1, :], jnp.where(row == 1, line[1:2, :], 0.0))
    for c, out in enumerate((out_own, out_sib)):
        at = slice(c * m, (c + 1) * m)
        out[:wide, :] = mm(dx_s[...], hot_s[:, at], TN).astype(out.dtype)
        out[wide:, :] = lines[:, at].astype(out.dtype)


def dx_chunk(info, own, from_x, from_y, far_a, far_b, dest, gate_w, up_w, line, extra, token):
    wide, f = gate_w.shape[1:]
    rows = far_a.shape[0]
    total = dest.shape[-1]
    return call(
        dx_kernel,
        [info, own, from_x, from_y, far_a, far_b, dest, gate_w, up_w, line],
        token,
        smem=1,
        out_specs=[IN_VMEM, IN_VMEM],
        scratch_shapes=[pltpu.VMEM((8 * rows, total), BF16), pltpu.VMEM((8 * rows, wide), BF16)],
        out_shape=[
            jax.ShapeDtypeStruct((wide + extra, total // 2), F32),
            jax.ShapeDtypeStruct((wide + extra, total // 2), BF16),
        ],
        cost_estimate=cost(2 * 8 * rows * (2 * f * wide + total * wide), 12e6),
        name="dx",
    )


def grads_kernel(n_chunk, is_in, info, *refs):
    halves, acts = refs[: 2 * n_chunk], refs[2 * n_chunk : 7 * n_chunk]
    n_out = 2 if is_in else 1
    outs = refs[7 * n_chunk : 7 * n_chunk + n_out]
    row_s, act_s, out_s, in_sems, out_sems = refs[7 * n_chunk + n_out :]
    rows = row_s.shape[1] // n_chunk
    cols = act_s.shape[2]
    f = cols // n_out
    col = pl.ds(0 if is_in else 2 * f, cols)
    wide = row_s.shape[2]
    half = pl.ds(0 if is_in else wide, wide)

    def loads(q):
        out = []
        for k in range(n_chunk):
            at = pl.ds(k * rows, rows)
            ref, lo = in_order(*acts[5 * k : 5 * k + 5])[q]
            src = halves[2 * k + q // 4].at[q % 4, :, half]
            out.append(pltpu.make_async_copy(src, row_s.at[q % 2, at], in_sems.at[q % 2, 2 * k]))
            src = ref.at[pl.ds(lo, rows), col]
            out.append(pltpu.make_async_copy(src, act_s.at[q % 2, at], in_sems.at[q % 2, 2 * k + 1]))
        return out

    def stores(q):
        return [
            pltpu.make_async_copy(out_s.at[q % 2, k], outs[k].at[info[q]], out_sems.at[q % 2, k])
            for k in range(n_out)
        ]

    for copy in loads(0):
        copy.start()
    for q in range(8):
        if q < 7:
            for copy in loads(q + 1):
                copy.start()
        for copy in loads(q):
            copy.wait()
        if q >= 2:
            for copy in stores(q - 2):
                copy.wait()
        if is_in:
            both = mm(row_s[q % 2], act_s[q % 2], TN)
            out_s[q % 2, 0] = both[:, :f]
            out_s[q % 2, 1] = both[:, f:]
        else:
            out_s[q % 2, 0] = mm(act_s[q % 2], row_s[q % 2], TN)
        for copy in stores(q):
            copy.start()
    for q in (6, 7):
        for copy in stores(q):
            copy.wait()


def grads(info, halves, acts, shapes):
    n_chunk = len(halves) // 2
    is_in = len(shapes) == 2
    rows, wide = halves[0].shape[1], halves[0].shape[2] // 2
    cols = acts[0].shape[1] // 3 * len(shapes)
    any_spec = pl.BlockSpec(memory_space=pl.ANY)
    return pl.pallas_call(
        functools.partial(grads_kernel, n_chunk, is_in),
        in_specs=[IN_SMEM] + [any_spec] * (7 * n_chunk),
        out_specs=[any_spec] * len(shapes),
        scratch_shapes=[
            pltpu.VMEM((2, n_chunk * rows, wide), BF16),
            pltpu.VMEM((2, n_chunk * rows, cols), BF16),
            pltpu.VMEM((2, len(shapes)) + shapes[0][1:], F32),
            pltpu.SemaphoreType.DMA((2, 2 * n_chunk)),
            pltpu.SemaphoreType.DMA((2, len(shapes))),
        ],
        out_shape=[jax.ShapeDtypeStruct(s, F32) for s in shapes],
        compiler_params=params(GRADS_LIMIT),
        cost_estimate=cost(1000 * 16 * n_chunk * rows * wide * cols, 2e10),
        name="grads_in" if is_in else "grads_out",
    )(info, *halves, *acts)


def join_kernel(info, *refs):
    out, table = refs[-2:]
    wide = out.shape[1] // (len(refs) - 2)
    for o, piece in enumerate(refs[:-2]):
        at = pl.ds(pl.multiple_of((info[8] ^ o) * wide, wide), wide)
        out[:, at] = piece[:wide, :].astype(F32).T.astype(BF16)
        table[info[8] ^ o] = piece[wide:, :].astype(F32)


def join(info, pieces, extra):
    wide, rows = pieces[0].shape[0] - extra, pieces[0].shape[1]
    return pl.pallas_call(
        join_kernel,
        in_specs=[IN_SMEM] + [IN_VMEM] * len(pieces),
        out_specs=[IN_VMEM] * 2,
        out_shape=[
            jax.ShapeDtypeStruct((rows, wide * len(pieces)), BF16),
            jax.ShapeDtypeStruct((len(pieces), extra, rows), F32),
        ],
        compiler_params=params(),
        name="join",
    )(info, *pieces)


def shards_rows(tokens, cotangent, routes, probs, slot_expert, gate_w, up_w, down_w):
    n_dp, n_exp = lax.axis_size("dp"), lax.axis_size("expert")
    local = gate_w.shape[0]
    tok = tokens.shape[0]
    n_chunk = n_exp // 2
    rows = 2 * n_dp * CAP
    n, e = lax.axis_index("dp"), lax.axis_index("expert")
    order = [3, 7, 1, 6, 2, 5, 0, 4]
    info = jnp.stack(
        [2 * (n ^ (k % 4)) + k // 4 for k in order]
        + [n, e * local, e % 2, e]
    ).astype(jnp.int32)

    def swap(a, o):
        return lax.ppermute(a, "dp", [(k, k ^ o) for k in range(n_dp)])

    def sibling(a):
        return lax.ppermute(a, "expert", [(k, k ^ 1) for k in range(n_exp)])

    def after(a, b):
        return lax.optimization_barrier((a, b))[0]

    def plane(a):
        return lax.ppermute(a, "expert", [(k, (k + 2) % n_exp) for k in range(n_exp)])

    last = info
    weights = (gate_w, up_w, down_w)
    sends = payload(info, tokens, cotangent, routes, probs, slot_expert, n_dp)
    pieces = [sends[0]] + [swap(sends[o], o) for o in range(1, n_dp)]
    own = stack(pieces, ready(weights, sends[0]))
    home, ring = None, None
    state = [dict() for _ in range(n_chunk)]

    def take(j):
        nonlocal last
        s = state[j]
        s["own"] = last = gate_on(s["came"], last)
        if j + 1 < n_chunk:
            state[j + 1]["came"] = plane(s["own"])

    def pair(j):
        state[j]["sib"] = sibling(state[j]["own"])

    def send(j):
        nonlocal last
        s = state[j]
        s["rows"], s["dest"], s["prob"], a3, b3, s["a1"], s["b2"] = partials(
            send_kernel, info, s["own"], s["sib"], weights, (), n_dp, last
        )
        s["a3"], s["b3"] = swap(a3, 1), swap(b3, 2)
        last = s["dest"]

    def keep(j):
        nonlocal last
        s = state[j]
        s["rows2"], s["keep"], s["weight"] = partials(
            keep_kernel, info, s["own"], s["sib"], weights, (s["dest"], s["prob"]), n_dp, last
        )
        last = s["weight"]

    def sums(j):
        nonlocal last
        s = state[j]
        to_x, to_y = second(s["keep"], s["a3"], s["b3"], s["a1"], s["b2"], last)
        s["to_x"], s["to_y"] = swap(to_x, 1), swap(to_y, 2)
        last = to_x

    def middle(j):
        nonlocal last
        s = state[j]
        s["act"], s["line"] = inner(s["keep"], s["to_x"], s["to_y"], s["weight"], s["dest"], last)
        s["x"], s["y"] = swap(s["act"], 1), swap(s["act"], 2)
        last = s["line"]

    def far(j):
        nonlocal last
        s = state[j]
        a, b = far_rows(s["x"], s["y"], last)
        s["far_a"], s["far_b"] = swap(a, 1), swap(b, 2)
        last = a

    def back(j):
        nonlocal home, ring, last
        s = state[j]
        s["acts"] = (s["act"], s["x"], s["y"], s["far_a"], s["far_b"])
        dx_own, dx_sib = dx_chunk(info, *s["acts"], s["dest"], gate_w, up_w, s["line"], 2 * n_exp, last)
        last = dx_own
        dx = dx_own + sibling(dx_sib).astype(F32)
        if j == 0:
            home = dx
        else:
            if ring is not None:
                dx = dx + ring.astype(F32)
            ring = plane(dx.astype(BF16))

    state[0]["own"] = own
    pair(0)
    state[1]["came"] = plane(after(own, state[0]["sib"]))
    send(0)
    keep(0)
    sums(0)
    middle(0)
    take(1)
    pair(1)
    send(1)
    keep(1)
    far(0)
    sums(1)
    take(2)
    pair(2)
    send(2)
    keep(2)
    middle(1)
    back(0)
    for j in range(2, n_chunk):
        sums(j)
        far(j - 1)
        if j + 1 < n_chunk:
            take(j + 1)
            pair(j + 1)
            send(j + 1)
            keep(j + 1)
        middle(j)
        back(j - 1)
    far(n_chunk - 1)
    back(n_chunk - 1)

    acts = [a for s in state for a in s["acts"]]
    got = [s[k] for s in state for k in ("rows", "rows2")]
    grad_gate, grad_up = grads(info, got, acts, [gate_w.shape, up_w.shape])
    home = (home + ring.astype(F32)).astype(BF16)
    pieces = [home[:, o * tok : (o + 1) * tok] for o in range(n_dp)]
    pieces = [pieces[0]] + [swap(pieces[o], o) for o in range(1, n_dp)]
    (grad_down,) = grads(info, got, acts, [down_w.shape])
    grad_tokens, flat = join(info, pieces, 2 * n_exp)
    flat = flat.astype(BF16)
    by_slot = flat.reshape(n_dp, n_exp, 2, tok).transpose(1, 0, 2, 3).reshape(n_exp * local, tok)
    match = routes[:, :, None] == slot_expert[None, None, :]
    grad_probs = jnp.sum(jnp.where(match, by_slot.T[:, None, :], jnp.zeros((), BF16)), axis=2)
    return (grad_tokens, grad_probs, grad_gate, grad_up, grad_down)


def forward_part(got_x, w_gate, w_up):
    gate = jnp.einsum("sekd,edf->sekf", got_x, w_gate, preferred_element_type=jnp.float32)
    upval = jnp.einsum("sekd,edf->sekf", got_x, w_up, preferred_element_type=jnp.float32)
    sig = jax.nn.sigmoid(gate)
    act = gate * sig
    hidden = (act * upval).astype(jnp.bfloat16)
    return (gate, upval, sig, act, hidden)


def shards_weights(tokens, cotangent, routes, probs, slot_expert, gate_w, up_w, down_w):
    n_exp = lax.axis_size("expert")
    local = gate_w.shape[0]
    tok_rows = tokens.shape[0]
    top = routes.shape[1]
    width = tokens.shape[1]
    count = local * n_exp
    rows_all = count * CAP
    flat = routes.reshape(-1)
    labels = jnp.arange(count, dtype=jnp.int32)
    match = slot_expert[None, :] == labels[:, None]
    slot_of = jnp.sum(jnp.where(match, labels[None, :], 0), axis=1)
    picked = flat[:, None] == labels[None, :]
    target = jnp.sum(jnp.where(picked, slot_of[None, :], 0), axis=1)
    hits = picked.astype(jnp.int32)
    position = jnp.sum((jnp.cumsum(hits, axis=0) - hits) * hits, axis=1)
    where_row = target * CAP + position
    placed = where_row[None, :] == jnp.arange(rows_all, dtype=jnp.int32)[:, None]
    token_map = jnp.any(placed.reshape(rows_all, tok_rows, top), axis=2).astype(jnp.bfloat16)
    send_x = jnp.dot(token_map, tokens, preferred_element_type=jnp.float32).astype(jnp.bfloat16)
    send_x = send_x.reshape(n_exp, local * CAP, width)
    send_dy = jnp.dot(token_map, cotangent, preferred_element_type=jnp.float32).astype(jnp.bfloat16)
    send_dy = send_dy.reshape(n_exp, local * CAP, width)
    zero_p = jnp.zeros((), jnp.bfloat16)
    send_p = jnp.sum(jnp.where(placed, probs.reshape(-1)[None, :], zero_p), axis=1).reshape(
        n_exp, local * CAP
    )
    w_gate, w_up, w_down = (
        lax.all_gather(gate_w, "dp", axis=1, tiled=True),
        lax.all_gather(up_w, "dp", axis=1, tiled=True),
        lax.all_gather(down_w, "dp", axis=2, tiled=True),
    )
    shape_rows = (n_exp, local, CAP, width)
    got_x = lax.all_to_all(send_x, "expert", split_axis=0, concat_axis=0, tiled=True).reshape(
        shape_rows
    )
    gate, upval, sig, act, hidden = forward_part(got_x, w_gate, w_up)
    got_dy, got_p = (
        lax.all_to_all(send_dy, "expert", split_axis=0, concat_axis=0, tiled=True),
        lax.all_to_all(send_p, "expert", split_axis=0, concat_axis=0, tiled=True),
    )
    got_dy = got_dy.reshape(shape_rows)
    weight = got_p.reshape(n_exp, local, CAP).astype(jnp.float32)[..., None]
    back = jnp.einsum("sekd,efd->sekf", got_dy, w_down, preferred_element_type=jnp.float32)
    dprob = jnp.sum(hidden.astype(jnp.float32) * back, axis=-1).astype(jnp.bfloat16)
    dh = weight * back
    d_gate = (dh * upval * sig * (1.0 + gate * (1.0 - sig))).astype(jnp.bfloat16)
    d_up = (dh * act).astype(jnp.bfloat16)
    dx_rows = (
        jnp.einsum("sekf,edf->sekd", d_gate, w_gate, preferred_element_type=jnp.float32)
        + jnp.einsum("sekf,edf->sekd", d_up, w_up, preferred_element_type=jnp.float32)
    ).astype(jnp.bfloat16)
    back_x, back_p = (
        lax.all_to_all(
            dx_rows.reshape(n_exp, local * CAP, width),
            "expert",
            split_axis=0,
            concat_axis=0,
            tiled=True,
        ),
        lax.all_to_all(
            dprob.reshape(n_exp, local * CAP), "expert", split_axis=0, concat_axis=0, tiled=True
        ),
    )
    wdy = (weight * got_dy.astype(jnp.float32)).astype(jnp.bfloat16)
    part_gate = jnp.einsum("sekd,sekf->edf", got_x, d_gate, preferred_element_type=jnp.float32)
    part_up = jnp.einsum("sekd,sekf->edf", got_x, d_up, preferred_element_type=jnp.float32)
    part_down = jnp.einsum("sekf,sekd->efd", hidden, wdy, preferred_element_type=jnp.float32)
    grad_gate, grad_up, grad_down = (
        lax.psum_scatter(part_gate, "dp", scatter_dimension=1, tiled=True),
        lax.psum_scatter(part_up, "dp", scatter_dimension=1, tiled=True),
        lax.psum_scatter(part_down, "dp", scatter_dimension=2, tiled=True),
    )
    returned_rows = back_x.reshape(rows_all, width)
    grad_tokens = lax.dot_general(
        token_map, returned_rows, (((0,), (0,)), ((), ())), preferred_element_type=jnp.float32
    ).astype(jnp.bfloat16)
    grad_probs = jnp.sum(jnp.where(placed, back_p.reshape(rows_all)[:, None], zero_p), axis=0)
    grad_probs = grad_probs.reshape(tok_rows, top)
    return (grad_tokens, grad_probs, grad_gate, grad_up, grad_down)


def solution(mesh):
    placed = (
        P(("dp", "expert"), None),
        P(("dp", "expert"), None),
        P(("dp", "expert"), None),
        P(("dp", "expert"), None),
        P(),
        P("expert", "dp", None),
        P("expert", "dp", None),
        P("expert", None, "dp"),
    )
    n_dp, n_exp = mesh.shape["dp"], mesh.shape["expert"]

    def shards(*args):
        local, rows = args[5].shape[0], 2 * n_dp * CAP
        by_rows = n_dp == 4 and local == 2 * n_dp and n_exp % 2 == 0 and n_exp >= 6 and rows % 16 == 0
        return (shards_rows if by_rows else shards_weights)(*args)

    return jax.shard_map(
        shards,
        mesh=mesh,
        in_specs=placed,
        out_specs=(
            P(("dp", "expert"), None),
            P(("dp", "expert"), None),
            P("expert", "dp", None),
            P("expert", "dp", None),
            P("expert", None, "dp"),
        ),
        check_vma=False,
    )
```
